256 devices in a mesh: px: 64 (over y_lo, z, x), py: 4 (over y_hi, core).
Axes of the slice: x: 4, y: 4 (y_hi: 2, y_lo: 2; y = y_hi * 2 + y_lo), z: 8, core: 2. Of those that a mesh axis runs over, the one named last changes fastest.
Arguments:
- features: bfloat16 [64, 128, 128, 128], P(None, 'px', 'py'), may hold values from -6 to 6
- cotangent: bfloat16 [64, 128, 128, 128], P(None, 'px', 'py'), may hold values from -6 to 6
- tucker_core: bfloat16 [2304, 2048], replicated, may hold values from -6 to 6
- in_factor: float32 [64, 48], replicated, may hold values from -0.875 to 0.875
- out_factor: float32 [64, 48], replicated, may hold values from -0.875 to 0.875
- x_factor: float32 [32, 16], replicated, may hold values from -1.5 to 1.5
- y_factor: float32 [32, 16], replicated, may hold values from -1.5 to 1.5
- z_factor: float32 [16, 8], replicated, may hold values from -2 to 2
Outputs:
- grad_features: bfloat16 [64, 128, 128, 128], P(None, 'px', 'py')
- grad_core: float32 [2304, 2048], P(('px', 'py'))
- grad_in: float32 [64, 48], replicated
- grad_out: float32 [64, 48], replicated
- grad_x: float32 [32, 16], replicated
- grad_y: float32 [32, 16], replicated
- grad_z: float32 [16, 8], replicated
The draws below stay inside these ranges and needn't reach their ends.
All inputs are finite; a program needn't handle non-finite values.
Results may differ from the reference program's by a relative error of at most 0.015.
Values may be sent and summed in bfloat16 or wider, within the bound.
A program may use at most 128 MiB of HBM per device.

```python
import math
import jax
import jax.numpy as jnp
from jax import lax

C = 64
NX = 128
NY = 128
NZ = 128
KX = 32
KY = 32
KZ = 16
RIN = 48
ROUT = 48
RX = 16
RY = 16
RZ = 8


def shard_levels(rng, dims, shards, smallest, top_value):
    gain, own = 1.0, jax.random.fold_in(rng, 6)
    for position, parts in shards:
        draws = jnp.exp(jax.random.uniform(jax.random.fold_in(own, position), (parts,), jnp.float32, smallest / len(shards), top_value / len(shards)))
        gain = gain * jnp.repeat(draws, dims[position] // parts).reshape([-1 if axis == position else 1 for axis in range(len(dims))])
    return gain


def scatter_about(own_key, shape, spread, most, cuts=(), dtype=jnp.bfloat16):
    entries = jax.random.normal(own_key, shape, jnp.float32) * spread
    if len(cuts) > 0:
        entries = shard_levels(own_key, shape, cuts, -0.22, 0.18) * entries
    return jnp.clip(entries, min=-most, max=most).astype(dtype)


def setup_inputs(seed: int = 0) -> dict:
    streams_of = jax.random.split(jax.random.key(seed), 9)
    return {
        "features": scatter_about(streams_of[0], (C, NX, NY, NZ), 1.0, 6.0, ((1, 64), (2, 4))),
        "cotangent": scatter_about(streams_of[1], (C, NX, NY, NZ), 1.0, 6.0, ((1, 64), (2, 4))),
        "tucker_core": scatter_about(streams_of[2], (RIN * ROUT, RX * RY * RZ), 1.0, 6.0),
        "in_factor": scatter_about(streams_of[3], (C, RIN), RIN ** -0.5, 0.875, (), jnp.float32),
        "out_factor": scatter_about(streams_of[4], (C, ROUT), ROUT ** -0.5, 0.875, (), jnp.float32),
        "x_factor": scatter_about(streams_of[5], (KX, RX), RX ** -0.5, 1.5, (), jnp.float32),
        "y_factor": scatter_about(streams_of[6], (KY, RY), RY ** -0.5, 1.5, (), jnp.float32),
        "z_factor": scatter_about(streams_of[7], (KZ, RZ), RZ ** -0.5, 2.0, (), jnp.float32),
    }


precise = lax.Precision.HIGHEST

def fourier_rows(count, length, offset, width):
    half = count // 2
    row_ids = lax.broadcasted_iota(jnp.int32, (count, width), 0)
    col_ids = lax.broadcasted_iota(jnp.int32, (count, width), 1) + offset
    freq = jnp.where(row_ids < half, row_ids, row_ids - half + 1)
    phase = freq * col_ids % length
    angle = phase.astype(jnp.float32) * (2.0 * math.pi / length)
    return jnp.where(row_ids < half, jnp.cos(angle), jnp.sin(angle)) * math.sqrt(2.0 / length)

def reference(features, cotangent, tucker_core, in_factor, out_factor, x_factor, y_factor, z_factor):
    x_basis = fourier_rows(KX, NX, 0, NX)
    y_basis = fourier_rows(KY, NY, 0, NY)
    z_basis = fourier_rows(KZ, NZ, 0, NZ)

    def analyse(values):
        z_part = jnp.einsum('cxyz,kz->cxyk', values.astype(jnp.float32), z_basis, precision=precise)
        yz_spec = jnp.einsum('cxyk,jy->xjkc', z_part, y_basis, precision=precise).astype(jnp.bfloat16)
        return jnp.einsum('xjkc,ax->ajkc', yz_spec.astype(jnp.float32), x_basis, precision=precise)
    spec_in = analyse(features)
    spec_out = analyse(cotangent)

    def tucker(core_full, fin, fout, fx, fy, fz):
        reshaped = core_full.reshape(RIN, ROUT, RX, RY, RZ)
        section = jnp.einsum('pqrst,ct->pqrsc', reshaped, fz, precision=precise)
        section = jnp.einsum('pqrsc,bs->pqrbc', section, fy, precision=precise)
        section = jnp.einsum('pqrbc,ar->pqabc', section, fx, precision=precise)
        section = jnp.einsum('pqabc,ip->iqabc', section, fin, precision=precise)
        return jnp.einsum('iqabc,oq->abcio', section, fout, precision=precise)
    weight, pull_back = jax.vjp(tucker, tucker_core.astype(jnp.float32), in_factor, out_factor, x_factor, y_factor, z_factor)
    grad_weight = spec_in[:, :, :, :, None] * spec_out[:, :, :, None, :]
    grads = pull_back(grad_weight)
    pulled = jnp.einsum('abcio,abco->abci', weight, spec_out, precision=precise)
    x_synth = jnp.einsum('abci,ax->xbci', pulled, x_basis, precision=precise).astype(jnp.bfloat16)
    y_synth = jnp.einsum('xbci,by->xyci', x_synth.astype(jnp.float32), y_basis, precision=precise)
    grad_features = jnp.einsum('xyci,cz->ixyz', y_synth, z_basis, precision=precise).astype(jnp.bfloat16)
    return (grad_features, grads[0], grads[1], grads[2], grads[3], grads[4], grads[5])
```

```python
import math

import jax
import jax.numpy as jnp
import numpy as np
from jax import lax
from jax.experimental import pallas as pl
from jax.experimental.pallas import tpu as pltpu
from jax.sharding import PartitionSpec as P

NX = 128
NY = 128
NZ = 128
KX = 32
KY = 32
KZ = 16
RIN = 48
ROUT = 48
RX = 16
RY = 16
RZ = 8
C = 64

BF = jnp.bfloat16
F32 = jnp.float32
MESH = pl.DeviceIdType.MESH
EXACT = lax.Precision.HIGHEST
NN = (((1,), (0,)), ((), ()))
NT = (((1,), (1,)), ((), ()))
TN = (((0,), (0,)), ((), ()))


def table(count, length):
    half = count // 2
    rows = np.arange(count)[:, None]
    cols = np.arange(length)[None, :]
    freq = np.where(rows < half, rows, rows - half + 1)
    angle = (freq * cols % length) * (2.0 * math.pi / length)
    values = np.where(rows < half, np.cos(angle), np.sin(angle)) * math.sqrt(2.0 / length)
    return values.astype(np.float32)


def two_parts(values):
    high = values.astype(jnp.bfloat16)
    low = (values - high.astype(np.float32)).astype(jnp.bfloat16)
    return high, low


def constants():
    ex, ey, ez = table(KX, NX), table(KY, NY), table(KZ, NZ)
    eye8 = np.eye(8, dtype=np.float32)
    strips = ey.reshape(KY, 4, 32).transpose(1, 0, 2)
    fwd = np.einsum("pjy,cd->pjcdy", strips, eye8).reshape(4, 256, 256)
    bwd = np.ascontiguousarray(fwd.transpose(0, 2, 1))
    z_high, z_low = two_parts(ez)
    z_rows = np.concatenate([z_high, z_low], 0)
    z_block = np.einsum("kz,ij->ikjz", z_high.astype(np.float32), eye8).reshape(128, 1024)
    planes = ex.reshape(KX, 2, 8, 4, 2)
    eye2 = np.eye(2, dtype=np.float32)
    gather = np.einsum("ayzxp,mn->pmaznyx", planes, eye2).reshape(2, 64, 128)
    gather = np.concatenate(two_parts(gather), 1)
    spread = np.einsum("ayzxp,mn->znyxpma", planes, eye2).reshape(128, 128)
    spread = np.concatenate(two_parts(spread), 0)
    swap = np.zeros((8, 2, 8, 8, 16), np.float32)
    for z in range(8):
        for n in range(2):
            for m in range(8):
                swap[z, n, m, m, 2 * z + n] = 1.0
    swap = swap.reshape(128, 128)
    rows36 = np.zeros((8, 48, 2, 192), np.float32)
    for m in range(8):
        for i in range(36):
            rows36[m, i, m // 4, (m % 4) * 36 + i] = 1.0
    rows9 = np.zeros((4, 80, 8, 48), np.float32)
    for p in range(4):
        for q in range(9):
            for j in range(8):
                rows9[p, q * 8 + j, j, p * 9 + q] = 1.0
    widen = np.zeros((RX, RZ, RX, RY, RZ), np.float32)
    for r in range(RX):
        for t in range(RZ):
            widen[r, t, r, :, t] = 1.0
    mats = (
        fwd, bwd, z_rows, z_block, gather, spread, swap, np.ascontiguousarray(swap.T),
        rows36.reshape(384, 384), rows9.reshape(320, 384), widen.reshape(128, 2048),
    )
    return [np.asarray(m).astype(jnp.bfloat16) for m in mats]


X_CORE, X_YHI, X_A_YX, X_A_Z, X_D_Z, X_C_Z, X_E_Z, X_D_YX, X_C_YX, X_E_YX, X_D_PY, X_C_PY, X_E_PY, X_E_BACK = range(14)


def iota(shape, dim):
    return lax.broadcasted_iota(jnp.int32, shape, dim)


def flag(mask):
    return jnp.where(mask, 1.0, 0.0).astype(F32)


def dot(a, b, dims=NN, precision=None):
    return lax.dot_general(a, b, dims, precision=precision, preferred_element_type=F32)


def kernel(
    feat, cot, core, fin, fout, fx, fy, fz,
    k_fwd, k_bwd, k_zrows, k_zblock, k_gather, k_spread, k_swap, k_swapt, k_rows36, k_rows9, k_widen,
    out_features, out_core, out_small,
    field, core_v, fin_v, fout_v, fx_v, fy_v, fz_v,
    fwd, bwd, zrows, zblock, gather, spread, swap, swapt, rows36, rows9, widen,
    yspec, part, core_in, yhi_out, yhi_in, a_out, a_in, az_out, az_in,
    modes, uvt, uvp, d_out, d_in, w_all, c_out, c_in, e_out, e_in,
    dy_out, dy_in, cy_out, cy_in, ey_out, ey_in, dp_out, dp_in, cp_in, ep_out, ep_in, eb_out, eb_in,
    zspec,
    local_sem, send_sem, recv_sem,
):
    px = lax.axis_index("px")
    py = lax.axis_index("py")
    x4 = lax.rem(px, 4)
    z = lax.rem(px // 4, 8)
    y_lo = px // 32
    yx = y_lo * 4 + x4
    y_hi = py // 2
    half = lax.rem(py, 2)

    def at_z(other):
        return (y_lo * 32 + other * 4 + x4, py)

    def at_yx(other):
        return (other // 4 * 32 + z * 4 + lax.rem(other, 4), py)

    def at_py(other):
        return (px, other)

    loads = []

    def load(src, dst):
        copy = pltpu.make_async_copy(src, dst, local_sem.at[len(loads)])
        copy.start()
        loads.append(copy)
        return copy

    get_fwd = load(k_fwd.at[py], fwd)
    get_field = [[load(src.at[:, plane], field.at[plane, f]) for f, src in enumerate((feat, cot))] for plane in range(2)]
    get_zrows = load(k_zrows, zrows)
    get_small = [load(s, d) for s, d in ((fin, fin_v), (fout, fout_v), (fx, fx_v), (fy, fy_v), (fz, fz_v))]
    get_swap = load(k_swap, swap)
    get_gather = load(k_gather, gather)
    get_core = load(core, core_v)
    get_spread = load(k_spread, spread)
    get_rows36 = load(k_rows36, rows36)
    get_swapt = load(k_swapt, swapt)
    get_rows9 = load(k_rows9, rows9)
    get_bwd = load(k_bwd.at[py], bwd)
    get_zblock = load(k_zblock, zblock)
    get_widen = load(k_widen, widen)

    barrier = pltpu.get_barrier_semaphore()
    for d in range(1, 8):
        pl.semaphore_signal(barrier, inc=1, device_id=at_z(lax.rem(z + d, 8)), device_id_type=MESH)
        pl.semaphore_signal(barrier, inc=1, device_id=at_yx(lax.rem(yx + d, 8)), device_id_type=MESH)
    for d in range(1, 4):
        pl.semaphore_signal(barrier, inc=1, device_id=at_py(lax.rem(py + d, 4)), device_id_type=MESH)

    sends = []

    def send(number, slot_out, slot_in, src, dst, device):
        copy = pltpu.make_async_remote_copy(
            src_ref=src, dst_ref=dst, send_sem=send_sem.at[number, slot_out],
            recv_sem=recv_sem.at[number, slot_in], device_id=device, device_id_type=MESH,
        )
        copy.start()
        sends.append(copy)

    def receive(number, slot, dst):
        pltpu.make_async_remote_copy(
            src_ref=dst, dst_ref=dst, send_sem=send_sem.at[number, slot],
            recv_sem=recv_sem.at[number, slot], device_id=at_py(lax.rem(py + 1, 4)), device_id_type=MESH,
        ).wait_recv()

    def exchange(number, src_of, into, mine, size, device_of):
        for d in range(1, size):
            other = lax.rem(mine + d, size)
            send(number, d, mine, src_of(other), into.at[mine], device_of(other))
        into[mine] = src_of(mine)[...]

    def arrive(number, into, mine, size):
        for d in range(1, size):
            other = lax.rem(mine + d, size)
            receive(number, other, into.at[other])

    get_fwd.wait()
    for plane in range(2):
        for f in range(2):
            get_field[plane][f].wait()

            def lines(i, carry, plane=plane, f=f):
                pair = []
                for h in range(2):
                    block = field[plane, f, pl.ds(i * 16 + h * 8, 8)].reshape(256, NZ)
                    pair.append(dot(fwd[...], block).reshape(KY, 8, NZ))
                rows = pl.ds(pl.multiple_of(plane * 128 + f * 64 + i * 16, 16), 16)
                yspec[:, rows, :] = jnp.concatenate(pair, axis=1).astype(BF)
                return carry

            lax.fori_loop(0, 4, lines, 0, unroll=True)
    get_zrows.wait()

    def depth(group):
        def one(i, carry):
            both = dot(zrows[...], yspec[group * 8 + i], NT)
            part[group, i] = (both[:KZ] + both[KZ:]).astype(BF)
            return carry

        lax.fori_loop(0, 8, one, 0, unroll=4)

    for h in range(2):
        depth(h * 2 + (1 - half))
    pl.semaphore_wait(barrier, 17)
    for h in range(2):
        send(X_CORE, h, h, part.at[h * 2 + (1 - half)], core_in.at[h], at_py(y_hi * 2 + (1 - half)))
    for h in range(2):
        depth(h * 2 + half)

    far = 1 - y_hi
    for h in range(2):
        receive(X_CORE, h, core_in.at[h])
    yhi_out[...] = (part[far * 2 + half].astype(F32) + core_in[far].astype(F32)).astype(BF)
    send(X_YHI, 0, 0, yhi_out, yhi_in, at_py(far * 2 + half))
    near = part[y_hi * 2 + half].astype(F32) + core_in[y_hi].astype(F32)

    for copy in get_small:
        copy.wait()
    fin_t = dot(fin_v[...], flag(lax.rem(iota((C, 128), 1), C) == iota((C, 128), 0)), NN, EXACT)
    fout_t = fout_v[...]
    b_mode = py * 8 + yx
    y_rows = dot(flag(iota((64, KY), 1) == b_mode), fy_v[...], NT, EXACT)
    z_rows = dot(flag(iota((64, KZ), 1) == 2 * z + iota((64, KZ), 0) // 32), fz_v[...], NT, EXACT)
    y_wide = flag(iota((RY, 128), 1) // RZ == iota((RY, 128), 0))
    z_wide = flag(lax.rem(iota((RZ, 128), 1), RZ) == iota((RZ, 128), 0))
    y_lane = dot(y_rows, y_wide, NN, EXACT)
    z_lane = dot(z_rows, z_wide, NN, EXACT)
    yz_lane = y_lane * z_lane
    x_rep = dot(flag(iota((64, KX), 1) == lax.rem(iota((64, KX), 0), KX)), fx_v[...], NT, EXACT)
    for r in range(RX):
        modes[:, r * 128:(r + 1) * 128] = (x_rep[:, r:r + 1] * yz_lane).astype(BF)
    x_cols = dot(fx_v[...], flag(lax.rem(iota((KX, 64), 1), KX) == iota((KX, 64), 0)), NN, EXACT)
    x_cols = jnp.concatenate([x_cols, x_cols], axis=0)
    x_cols = jnp.where(iota((32, 64), 0) // RX == iota((32, 64), 1) // KX, x_cols, 0.0)
    x_high = x_cols.astype(BF)
    x_parts = jnp.concatenate([x_cols, x_cols - x_high.astype(F32)], axis=0).astype(BF)
    z_taps = dot(flag(iota((256, KZ), 0) // RX == iota((256, KZ), 1)), fz_v[...], NT, EXACT)
    z_taps = dot(z_taps, z_wide, NN, EXACT)
    z_taps = jnp.where(lax.rem(iota((256, 128), 0), RX) == iota((256, 128), 1) // RZ, z_taps, 0.0)
    z_high = z_taps.astype(BF)
    z_parts = jnp.concatenate([z_taps, z_taps - z_high.astype(F32)], axis=1).astype(BF)
    y_taps = dot(fy_v[...], y_wide, TN, EXACT)
    for block in range(8):
        for m in range(2):
            uvp[block, m * 192 + 144:(m + 1) * 192, :] = jnp.zeros((48, 64), BF)

    receive(X_YHI, 0, yhi_in)
    a_out[...] = (near + yhi_in[...].astype(F32)).astype(BF)

    exchange(X_A_YX, lambda o: a_out.at[o], a_in, yx, 8, at_yx)
    get_swap.wait()
    arrive(X_A_YX, a_in, yx, 8)
    az_out[...] = dot(swap[...], a_in[...].reshape(128, 256)).astype(BF).reshape(8, 16, 256)
    exchange(X_A_Z, lambda o: az_out.at[o], az_in, z, 8, at_z)
    get_gather.wait()
    arrive(X_A_Z, az_in, z, 8)
    slabs = az_in[...].reshape(128, 256)
    both = dot(gather[0], slabs[:, :128]) + dot(gather[1], slabs[:, 128:])
    spec = both[:64] + both[64:]
    spec_t = spec.T
    in_t, out_t = spec_t[:C], spec_t[C:]

    u_t = dot(fin_t[:, :C], in_t, NN, EXACT)
    v_t = dot(fout_t, out_t, NN, EXACT)
    for g in range(16):
        rows = u_t[g * 3:(g + 1) * 3][:, None, :] * v_t[None, :, :]
        rows = rows.reshape(144, 64)
        uvt[g * 144:(g + 1) * 144, :] = rows
        uvp[g % 8, (g // 8) * 192:(g // 8) * 192 + 144, :] = rows.astype(BF)
    for g in range(8):
        flow = dot(x_parts, uvp[g], NT)
        d_out[g] = (flow[:32] + flow[32:]).astype(BF)
    exchange(X_D_Z, lambda o: d_out.at[o], d_in, z, 8, at_z)

    get_core.wait()
    for g in range(8):
        w_all[g * 6:(g + 1) * 6] = dot(core_v[g * 288:(g + 1) * 288, :], modes[...], NT).reshape(6, 48, 64)
    weight = w_all[...]
    h_t = jnp.sum(weight * v_t[None, :, :], axis=1)
    pulled = dot(h_t, fin_t, TN, EXACT)
    lane = iota((64, 128), 1)
    pulled = jnp.concatenate(
        [jnp.where(lane < C, pulled, 0.0), jnp.where(lane >= C, pulled, 0.0)], axis=0
    ).astype(BF)
    get_spread.wait()
    synth = dot(spread[...], pulled)
    c_out[...] = (synth[:128] + synth[128:]).astype(BF).reshape(8, 16, 128)
    exchange(X_C_Z, lambda o: c_out.at[o], c_in, z, 8, at_z)

    g_t = jnp.sum(weight * u_t[:, None, :], axis=0)
    uv = uvt[...].T.astype(BF)
    acc = jnp.zeros((64, 128), F32)
    yz_sum = jnp.zeros((64, 128), F32)
    for g in range(8):
        flow = dot(uv, core_v[:, g * 256:(g + 1) * 256])
        for h in range(2):
            r = g * 2 + h
            piece = flow[:, h * 128:(h + 1) * 128]
            acc = acc + jnp.where(lane == 96 + r, jnp.sum(piece * yz_lane, axis=1, keepdims=True), 0.0)
            yz_sum = yz_sum + piece * x_rep[:, r:r + 1]
    row = iota((64, 128), 0)
    small = jnp.concatenate([acc[:32] + acc[32:], jnp.zeros((32, 128), F32)], axis=0)
    y_sum = jnp.sum(yz_sum * z_lane, axis=0, keepdims=True)
    z_sum = yz_sum * y_lane
    z_sum = [jnp.sum(z_sum[n * 32:(n + 1) * 32], axis=0, keepdims=True) for n in range(2)]
    sums = jnp.concatenate([y_sum, z_sum[0], z_sum[1], jnp.zeros((5, 128), F32)], axis=0)
    y_place = flag(iota((128, 128), 1) == 96 + iota((128, 128), 0) // RZ)
    z_place = flag(iota((128, 128), 1) == 112 + lax.rem(iota((128, 128), 0), RZ))
    y_put = dot(sums, y_place, NN, EXACT)
    z_put = dot(sums, z_place, NN, EXACT)
    small = small + jnp.where(row == 32 + b_mode, y_put[0:1], 0.0)
    small = small + jnp.where(row == 2 * z, z_put[1:2], 0.0) + jnp.where(row == 2 * z + 1, z_put[2:3], 0.0)
    h_pad = jnp.concatenate([h_t, jnp.zeros((80, 64), F32)], axis=0)
    g_pad = jnp.concatenate([jnp.zeros((48, 64), F32), g_t, jnp.zeros((32, 64), F32)], axis=0)
    small = small + dot(in_t, h_pad, NT, EXACT) + dot(out_t, g_pad, NT, EXACT)
    e_out[...] = small.reshape(8, 8, 128)
    exchange(X_E_Z, lambda o: e_out.at[o], e_in, z, 8, at_z)

    arrive(X_D_Z, d_in, z, 8)
    taps = dot(d_in[...].reshape(256, 384), z_parts, TN)
    taps = (taps[:, :128] + taps[:, 128:]).astype(BF)
    get_rows36.wait()
    dy_out[...] = dot(rows36[...], taps).astype(BF).reshape(8, 48, 128)
    exchange(X_D_YX, lambda o: dy_out.at[o], dy_in, yx, 8, at_yx)

    get_swapt.wait()
    arrive(X_C_Z, c_in, z, 8)
    cy_out[...] = dot(swapt[...], c_in[...].reshape(128, 128)).astype(BF).reshape(8, 16, 128)
    exchange(X_C_YX, lambda o: cy_out.at[o], cy_in, yx, 8, at_yx)

    arrive(X_E_Z, e_in, z, 8)
    ey_out[...] = jnp.sum(e_in[...], axis=0)
    exchange(X_E_YX, lambda o: ey_out, ey_in, yx, 8, at_yx)

    arrive(X_C_YX, cy_in, yx, 8)
    exchange(X_C_PY, lambda o: cy_in, cp_in, py, 4, at_py)
    get_rows9.wait()
    arrive(X_D_YX, dy_in, yx, 8)
    dp_out[...] = dot(rows9[...], dy_in[...].reshape(384, 128)).astype(BF).reshape(4, 80, 128)
    exchange(X_D_PY, lambda o: dp_out.at[o], dp_in, py, 4, at_py)
    arrive(X_E_YX, ey_in, yx, 8)
    ep_out[...] = jnp.sum(ey_in[...], axis=0)
    exchange(X_E_PY, lambda o: ep_out, ep_in, py, 4, at_py)

    get_bwd.wait()
    get_zblock.wait()
    arrive(X_C_PY, cp_in, py, 4)
    for g in range(4):
        deep = dot(cp_in[g].reshape(128, 128), zblock[...], TN)
        for i in range(4):
            pair = [deep[:, (2 * i + h) * 128:(2 * i + h + 1) * 128].reshape(16, 8, 128) for h in range(2)]
            zspec[:, g * 64 + i * 16:g * 64 + (i + 1) * 16, :] = jnp.concatenate(pair, axis=1).astype(BF)

    arrive(X_E_PY, ep_in, py, 4)
    eb_out[...] = jnp.sum(ep_in[...], axis=0)
    exchange(X_E_BACK, lambda o: eb_out, eb_in, z, 8, at_z)

    for plane in range(2):
        for i in range(8):
            lines = dot(bwd[...], zspec[plane * 8 + i])
            out_features[plane, i * 8:(i + 1) * 8] = lines.reshape(8, 32, 128).astype(BF)

    get_widen.wait()
    arrive(X_D_PY, dp_in, py, 4)
    rows = dp_in[...].reshape(320, 128)
    y_taps = y_taps.reshape(4, 1, 8, 128)
    for r in range(RX):
        wide = dot(rows, widen[:, r * 128:(r + 1) * 128]).reshape(4, 10, 8, 128) * y_taps
        out_core[:, r * 128:(r + 1) * 128] = jnp.sum(jnp.sum(wide, axis=0), axis=1)[:9]

    arrive(X_E_BACK, eb_in, z, 8)
    out_small[...] = eb_in[...].reshape(64, 128).T
    for copy in sends:
        copy.wait_send()


def write_out(planes, core_rows, small, features, core, g_in, g_out, g_x, g_y, g_z, x_v, y_v, z_v, sem):
    copies = [pltpu.make_async_copy(planes.at[i], features.at[:, i], sem.at[i]) for i in range(2)]
    copies.append(pltpu.make_async_copy(core_rows, core, sem.at[2]))
    copies.append(pltpu.make_async_copy(small.at[0:48], g_in, sem.at[3]))
    copies.append(pltpu.make_async_copy(small.at[48:96], g_out, sem.at[4]))
    for copy in copies:
        copy.start()
    x_v[...] = small[96:112, 0:32]
    y_v[...] = small[96:112, 32:64]
    z_v[...] = small[112:120, 0:16]
    for i, (src, dst) in enumerate(((x_v, g_x), (y_v, g_y), (z_v, g_z))):
        copies.append(pltpu.make_async_copy(src, dst, sem.at[5 + i]))
        copies[-1].start()
    for copy in copies:
        copy.wait()


def shards(features, cotangent, tucker_core, in_factor, out_factor, x_factor, y_factor, z_factor):
    tables = [jnp.asarray(m) for m in constants()]
    hbm = pl.BlockSpec(memory_space=pltpu.HBM)
    vmem = pl.BlockSpec(memory_space=pltpu.VMEM)
    buffers = [
        ((2, 2, 64, 32, 128), BF), ((2304, 2048), BF), ((48, 64), F32), ((48, 64), F32), ((16, 32), F32),
        ((16, 32), F32), ((8, 16), F32),
        ((256, 256), BF), ((256, 256), BF), ((32, 128), BF), ((128, 1024), BF), ((2, 128, 128), BF),
        ((256, 128), BF), ((128, 128), BF), ((128, 128), BF), ((384, 384), BF), ((320, 384), BF), ((128, 2048), BF),
        ((32, 256, 128), BF), ((4, 8, 16, 256), BF), ((2, 8, 16, 256), BF), ((8, 16, 256), BF), ((8, 16, 256), BF),
        ((8, 16, 256), BF), ((8, 16, 256), BF), ((8, 16, 256), BF), ((8, 16, 256), BF),
        ((64, 2048), BF), ((2304, 64), F32), ((8, 384, 64), BF), ((8, 32, 384), BF), ((8, 32, 384), BF),
        ((48, 48, 64), F32), ((8, 16, 128), BF), ((8, 16, 128), BF), ((8, 8, 128), F32), ((8, 8, 128), F32),
        ((8, 48, 128), BF), ((8, 48, 128), BF), ((8, 16, 128), BF), ((8, 16, 128), BF),
        ((8, 128), F32), ((8, 8, 128), F32), ((4, 80, 128), BF), ((4, 80, 128), BF), ((4, 8, 16, 128), BF),
        ((8, 128), F32), ((4, 8, 128), F32), ((8, 128), F32), ((8, 8, 128), F32),
        ((16, 256, 128), BF),
    ]
    factors = (in_factor, out_factor, x_factor, y_factor, z_factor)
    operands = [features, cotangent, tucker_core] + [a.T for a in factors] + tables
    planes, core_rows, small = pl.pallas_call(
        kernel,
        out_shape=(
            jax.ShapeDtypeStruct((2, C, 32, NZ), BF),
            jax.ShapeDtypeStruct((9, 2048), F32),
            jax.ShapeDtypeStruct((128, 64), F32),
        ),
        in_specs=[hbm] * (8 + len(tables)),
        out_specs=(vmem, vmem, vmem),
        scratch_shapes=[pltpu.VMEM(shape, dtype) for shape, dtype in buffers] + [
            pltpu.SemaphoreType.DMA((24,)),
            pltpu.SemaphoreType.DMA((14, 8)),
            pltpu.SemaphoreType.DMA((14, 8)),
        ],
        compiler_params=pltpu.CompilerParams(
            collective_id=0, has_side_effects=True, vmem_limit_bytes=32 * 1024 * 1024
        ),
    )(*[pltpu.with_memory_space_constraint(a, pltpu.HBM) for a in operands])
    outs = pl.pallas_call(
        write_out,
        out_shape=(
            jax.ShapeDtypeStruct((C, 2, 32, NZ), BF),
            jax.ShapeDtypeStruct((9, 2048), F32),
            jax.ShapeDtypeStruct((RIN, C), F32),
            jax.ShapeDtypeStruct((ROUT, C), F32),
            jax.ShapeDtypeStruct((RX, KX), F32),
            jax.ShapeDtypeStruct((RY, KY), F32),
            jax.ShapeDtypeStruct((RZ, KZ), F32),
        ),
        in_specs=[vmem] * 3,
        out_specs=[hbm] * 7,
        scratch_shapes=[
            pltpu.VMEM((RX, KX), F32), pltpu.VMEM((RY, KY), F32), pltpu.VMEM((RZ, KZ), F32),
            pltpu.SemaphoreType.DMA((8,)),
        ],
    )(planes, core_rows, small)
    return outs[0], outs[1], outs[2].T, outs[3].T, outs[4].T, outs[5].T, outs[6].T


def solution(mesh):
    placed = (P(None, "px", "py", None), P(None, "px", "py", None), P(), P(), P(), P(), P(), P())
    return jax.shard_map(
        shards,
        mesh=mesh,
        in_specs=placed,
        out_specs=(P(None, "px", "py", None), P(("px", "py"), None), P(), P(), P(), P(), P()),
        check_vma=False,
    )
```

```python
import math

import jax
import jax.numpy as jnp
import numpy as np
from jax import lax
from jax.experimental import pallas as pl
from jax.experimental.pallas import tpu as pltpu
from jax.sharding import PartitionSpec as P

NX = 128
NY = 128
NZ = 128
KX = 32
KY = 32
KZ = 16
RIN = 48
ROUT = 48
RX = 16
RY = 16
RZ = 8
C = 64

BF = jnp.bfloat16
F32 = jnp.float32
MESH = pl.DeviceIdType.MESH
EXACT = lax.Precision.HIGHEST
NN = (((1,), (0,)), ((), ()))
NT = (((1,), (1,)), ((), ()))
TN = (((0,), (0,)), ((), ()))


def table(count, length):
    half = count // 2
    rows = np.arange(count)[:, None]
    cols = np.arange(length)[None, :]
    freq = np.where(rows < half, rows, rows - half + 1)
    angle = (freq * cols % length) * (2.0 * math.pi / length)
    values = np.where(rows < half, np.cos(angle), np.sin(angle)) * math.sqrt(2.0 / length)
    return values.astype(np.float32)


def two_parts(values):
    high = values.astype(jnp.bfloat16)
    low = (values - high.astype(np.float32)).astype(jnp.bfloat16)
    return high, low


def constants():
    ex, ey, ez = table(KX, NX), table(KY, NY), table(KZ, NZ)
    eye8 = np.eye(8, dtype=np.float32)
    strips = ey.reshape(KY, 4, 32).transpose(1, 0, 2)
    fwd = np.einsum("pjy,cd->pjcdy", strips, eye8).reshape(4, 256, 256)
    bwd = np.ascontiguousarray(fwd.transpose(0, 2, 1))
    z_high, z_low = two_parts(ez)
    z_rows = np.concatenate([z_high, z_low], 0)
    z_block = np.einsum("kz,ij->ikjz", z_high.astype(np.float32), eye8).reshape(128, 1024)
    planes = ex.reshape(KX, 2, 8, 4, 2)
    eye2 = np.eye(2, dtype=np.float32)
    gather = np.einsum("ayzxp,mn->pmaznyx", planes, eye2).reshape(2, 64, 128)
    gather = np.concatenate(two_parts(gather), 1)
    spread = np.einsum("ayzxp,mn->znyxpma", planes, eye2).reshape(128, 128)
    spread = np.concatenate(two_parts(spread), 0)
    swap = np.zeros((8, 2, 8, 8, 16), np.float32)
    for z in range(8):
        for n in range(2):
            for m in range(8):
                swap[z, n, m, m, 2 * z + n] = 1.0
    swap = swap.reshape(128, 128)
    swap_add = np.concatenate([swap, swap], 1)
    rows9 = np.zeros((2, 8, 2, 16, 2, 192), np.float32)
    for h in range(2):
        for m in range(8):
            for c in range(2):
                for q in range(9):
                    rows9[h, m, c, q, m // 4, (m % 4) * 36 + (h * 2 + c) * 9 + q] = 1.0
    widen = np.zeros((RX, RZ, RX, RY, RZ), np.float32)
    for r in range(RX):
        for t in range(RZ):
            widen[r, t, r, :, t] = 1.0
    mats = (
        fwd, bwd, z_rows, z_block, gather, spread, swap_add, np.ascontiguousarray(swap.T),
        rows9.reshape(512, 384), widen.reshape(128, 2048),
    )
    return [np.asarray(m).astype(jnp.bfloat16) for m in mats]


(
    X_A_CORE, X_A_XY, X_A_Z, X_D_Z, X_C_Z, X_D_XY, X_C_XY, X_D_CORE, X_C_CORE,
    X_G_SPLIT, X_G_Z, X_G_X, X_G_Y, X_G_CORE, X_F_Z, X_F_X, X_F_Y, X_F_CORE,
) = range(18)


def iota(shape, dim):
    return lax.broadcasted_iota(jnp.int32, shape, dim)


def flag(mask):
    return jnp.where(mask, 1.0, 0.0).astype(F32)


def dot(a, b, dims=NN, precision=None):
    return lax.dot_general(a, b, dims, precision=precision, preferred_element_type=F32)


def kernel(
    feat, cot, core, fin, fout, fx, fy, fz,
    k_fwd, k_bwd, k_zrows, k_zblock, k_gather, k_spread, k_swap, k_swapt, k_rows9, k_widen,
    out_features, out_core, out_pair, out_modes,
    field, core_v, fin_v, fout_v, fx_v, fy_v, fz_v,
    fwd, bwd, zrows, zblock, gather, spread, swap, swapt, rows9, widen,
    yspec, part, core_in, a_out, a_in, az_out, az_in,
    modes, uvt, uvp, d_out, d_in, w_all, c_out, c_in,
    g_out, gs_in, gz_out, gz_in, gx_out, gx_in, gy_out, gy_in, gc_out, gc_in,
    f_out, fz_in, fx_out, fx_in, fy_out, fy_in, fc_out, fc_in,
    dy_out, dy_in, dc_in, cy_out, cp_in,
    zspec, local_sem, send_sem, recv_sem,
):
    px = lax.axis_index("px")
    py = lax.axis_index("py")
    x4 = lax.rem(px, 4)
    z = lax.rem(px // 4, 8)
    y_lo = px // 32
    yx = y_lo * 4 + x4
    y_hi = py // 2
    half = lax.rem(py, 2)
    y = y_hi * 2 + y_lo
    xy = y * 4 + x4
    other_core = (px, y_hi * 2 + 1 - half)

    def at_z(other):
        return (y_lo * 32 + other * 4 + x4, py)

    def at_xy(other):
        there = lax.rem(other, 8)
        return (there // 4 * 32 + z * 4 + lax.rem(there, 4), other // 8 * 2 + half)

    def at_x(other):
        return (y_lo * 32 + z * 4 + other, py)

    def at_y(other):
        return (lax.rem(other, 2) * 32 + z * 4 + x4, other // 2 * 2 + half)

    along_z = [lax.rem(z + d, 8) for d in (4, 3, 5, 2, 6, 1, 7)]
    along_x = [lax.rem(x4 + d, 4) for d in (2, 1, 3)]
    along_y = [lax.rem(y + d, 4) for d in (2, 1, 3)]
    along_xy = [
        lax.rem(y + dy, 4) * 4 + lax.rem(x4 + dx, 4)
        for dy, dx in (
            (2, 2), (2, 1), (2, 3), (1, 2), (3, 2), (2, 0), (0, 2), (1, 1),
            (1, 3), (3, 1), (3, 3), (1, 0), (3, 0), (0, 1), (0, 3),
        )
    ]

    loads = []

    def load(src, dst):
        copy = pltpu.make_async_copy(src, dst, local_sem.at[len(loads)])
        copy.start()
        loads.append(copy)
        return copy

    get_fwd = load(k_fwd.at[py], fwd)
    get_field = [
        [load(src.at[i * 16:(i + 1) * 16], field.at[f, i * 16:(i + 1) * 16]) for f, src in enumerate((feat, cot))]
        for i in range(4)
    ]

    barrier = pltpu.get_barrier_semaphore()
    for other in along_z:
        pl.semaphore_signal(barrier, inc=1, device_id=at_z(other), device_id_type=MESH)
    for other in along_xy:
        pl.semaphore_signal(barrier, inc=1, device_id=at_xy(other), device_id_type=MESH)
    pl.semaphore_signal(barrier, inc=1, device_id=other_core, device_id_type=MESH)

    get_zrows = load(k_zrows, zrows)
    get_small = [load(s, d) for s, d in ((fin, fin_v), (fout, fout_v), (fx, fx_v), (fy, fy_v), (fz, fz_v))]
    get_swap = load(k_swap, swap)
    get_gather = load(k_gather, gather)
    get_core = load(core, core_v)
    get_spread = load(k_spread, spread)
    get_rows9 = load(k_rows9, rows9)
    get_swapt = load(k_swapt, swapt)
    get_zblock = load(k_zblock, zblock)
    get_bwd = load(k_bwd.at[py], bwd)
    get_widen = load(k_widen, widen)

    sends = []

    def send(number, slot_out, slot_in, src, dst, device):
        copy = pltpu.make_async_remote_copy(
            src_ref=src, dst_ref=dst, send_sem=send_sem.at[number, slot_out],
            recv_sem=recv_sem.at[number, slot_in], device_id=device, device_id_type=MESH,
        )
        copy.start()
        sends.append(copy)

    def receive(number, slot, dst):
        pltpu.make_async_remote_copy(
            src_ref=dst, dst_ref=dst, send_sem=send_sem.at[number, slot],
            recv_sem=recv_sem.at[number, slot], device_id=other_core, device_id_type=MESH,
        ).wait_recv()

    def exchange(number, src_of, into, mine, others, device_of):
        for d, other in enumerate(others):
            send(number, d, mine, src_of(other), into.at[mine], device_of(other))
        into[mine] = src_of(mine)[...]

    def arrive(number, into, others):
        for other in others[::-1]:
            receive(number, other, into.at[other])

    get_fwd.wait()
    for i in range(4):
        for f in range(2):
            get_field[i][f].wait()

            def lines(plane, carry, i=i, f=f):
                pair = []
                for h in range(2):
                    c = i * 16 + h * 8
                    block = field[f, c:c + 8, plane].reshape(256, NZ)
                    pair.append(dot(fwd[...], block).reshape(KY, 8, NZ))
                rows = pl.ds(pl.multiple_of(plane * 128 + f * 64 + i * 16, 16), 16)
                yspec[:, rows, :] = jnp.concatenate(pair, axis=1).astype(BF)
                return carry

            lax.fori_loop(0, 2, lines, 0, unroll=True)
    get_zrows.wait()

    def depth(group):
        def one(i, carry):
            both = dot(zrows[...], yspec[group * 8 + i], NT)
            part[group, i] = (both[:KZ] + both[KZ:]).astype(BF)
            return carry

        lax.fori_loop(0, 8, one, 0, unroll=4)

    for h in range(2):
        depth(h * 2 + (1 - half))
    pl.semaphore_wait(barrier, 23)
    for h in range(2):
        send(X_A_CORE, h, h, part.at[h * 2 + (1 - half)], core_in.at[h], other_core)
    for h in range(2):
        depth(h * 2 + half)

    for h in range(2):
        receive(X_A_CORE, h, core_in.at[h])
        a_out[h * 8:(h + 1) * 8] = (part[h * 2 + half].astype(F32) + core_in[h].astype(F32)).astype(BF)
    exchange(X_A_XY, lambda o: a_out.at[o], a_in, xy, along_xy, at_xy)

    for copy in get_small:
        copy.wait()
    fin_t = dot(fin_v[...], flag(lax.rem(iota((C, 128), 1), C) == iota((C, 128), 0)), NN, EXACT)
    fout_t = fout_v[...]
    b_mode = py * 8 + yx
    y_rows = dot(flag(iota((64, KY), 1) == b_mode), fy_v[...], NT, EXACT)
    z_rows = dot(flag(iota((64, KZ), 1) == 2 * z + iota((64, KZ), 0) // 32), fz_v[...], NT, EXACT)
    y_wide = flag(iota((RY, 128), 1) // RZ == iota((RY, 128), 0))
    z_wide = flag(lax.rem(iota((RZ, 128), 1), RZ) == iota((RZ, 128), 0))
    y_lane = dot(y_rows, y_wide, NN, EXACT)
    z_lane = dot(z_rows, z_wide, NN, EXACT)
    yz_lane = y_lane * z_lane
    x_rep = dot(flag(iota((64, KX), 1) == lax.rem(iota((64, KX), 0), KX)), fx_v[...], NT, EXACT)
    for r in range(RX):
        modes[:, r * 128:(r + 1) * 128] = (x_rep[:, r:r + 1] * yz_lane).astype(BF)
    x_cols = dot(fx_v[...], flag(lax.rem(iota((KX, 64), 1), KX) == iota((KX, 64), 0)), NN, EXACT)
    x_cols = jnp.concatenate([x_cols, x_cols], axis=0)
    x_cols = jnp.where(iota((32, 64), 0) // RX == iota((32, 64), 1) // KX, x_cols, 0.0)
    x_high = x_cols.astype(BF)
    x_parts = jnp.concatenate([x_cols, x_cols - x_high.astype(F32)], axis=0).astype(BF)
    z_taps = dot(flag(iota((256, KZ), 0) // RX == iota((256, KZ), 1)), fz_v[...], NT, EXACT)
    z_taps = dot(z_taps, z_wide, NN, EXACT)
    z_taps = jnp.where(lax.rem(iota((256, 128), 0), RX) == iota((256, 128), 1) // RZ, z_taps, 0.0)
    z_high = z_taps.astype(BF)
    z_parts = jnp.concatenate([z_taps, z_taps - z_high.astype(F32)], axis=1).astype(BF)
    y_taps = dot(fy_v[...], y_wide, TN, EXACT)
    for block in range(8):
        for m in range(2):
            uvp[block, m * 192 + 144:(m + 1) * 192, :] = jnp.zeros((48, 64), BF)

    get_swap.wait()
    arrive(X_A_XY, a_in, along_xy)
    az_out[...] = dot(swap[...], a_in[...].reshape(256, 256)).astype(BF).reshape(8, 16, 256)
    exchange(X_A_Z, lambda o: az_out.at[o], az_in, z, along_z, at_z)

    get_core.wait()
    for g in range(8):
        w_all[g * 6:(g + 1) * 6] = dot(core_v[g * 288:(g + 1) * 288, :], modes[...], NT).reshape(6, 48, 64)

    get_gather.wait()
    arrive(X_A_Z, az_in, along_z)
    slabs = az_in[...].reshape(128, 256)
    both = dot(gather[0], slabs[:, :128]) + dot(gather[1], slabs[:, 128:])
    spec = both[:64] + both[64:]
    spec_t = spec.T

    u_t = dot(fin_t[:, :C], spec_t[:C], NN, EXACT)
    v_t = dot(fout_t, spec_t[C:], NN, EXACT)
    for g in range(16):
        rows = u_t[g * 3:(g + 1) * 3][:, None, :] * v_t[None, :, :]
        rows = rows.reshape(144, 64)
        uvt[g * 144:(g + 1) * 144, :] = rows
        uvp[g % 8, (g // 8) * 192:(g // 8) * 192 + 144, :] = rows.astype(BF)
    for g in range(8):
        flow = dot(x_parts, uvp[g], NT)
        d_out[g] = (flow[:32] + flow[32:]).astype(BF)
    exchange(X_D_Z, lambda o: d_out.at[o], d_in, z, along_z, at_z)

    weight = w_all[...]
    h_t = jnp.sum(weight * v_t[None, :, :], axis=1)
    pulled = dot(h_t, fin_t, TN, EXACT)
    lane = iota((64, 128), 1)
    pulled = jnp.concatenate(
        [jnp.where(lane < C, pulled, 0.0), jnp.where(lane >= C, pulled, 0.0)], axis=0
    ).astype(BF)
    get_spread.wait()
    synth = dot(spread[...], pulled)
    c_out[...] = (synth[:128] + synth[128:]).astype(BF).reshape(8, 16, 128)
    exchange(X_C_Z, lambda o: c_out.at[o], c_in, z, along_z, at_z)

    g_t = jnp.sum(weight * u_t[:, None, :], axis=0)
    for f, ranks in enumerate((h_t, g_t)):
        grad = dot(ranks, spec[:, f * C:(f + 1) * C], NN, EXACT)
        g_out[f] = jnp.concatenate([grad[:24], grad[24:]], axis=1)
    send(X_G_SPLIT, 0, 0, g_out.at[1 - half], gs_in, other_core)

    uv = uvt[...].T.astype(BF)
    x_sum = jnp.zeros((64, 128), F32)
    yz_sum = jnp.zeros((64, 128), F32)
    for g in range(8):
        flow = dot(uv, core_v[:, g * 256:(g + 1) * 256])
        for h in range(2):
            r = g * 2 + h
            piece = flow[:, h * 128:(h + 1) * 128]
            x_sum = x_sum + jnp.where(lane == r, jnp.sum(piece * yz_lane, axis=1, keepdims=True), 0.0)
            yz_sum = yz_sum + piece * x_rep[:, r:r + 1]
    row16 = iota((16, 128), 0)
    lane16 = iota((16, 128), 1)
    modes_grad = dot(
        flag(iota((16, 128), 0) == iota((16, 128), 1)), x_sum[:32] + x_sum[32:], NT, EXACT
    )
    modes_grad = jnp.concatenate([modes_grad, jnp.zeros((16, 96), F32)], axis=1)
    y_sum = jnp.sum(yz_sum * z_lane, axis=0, keepdims=True)
    y_pick = flag(iota((16, 128), 1) // RZ == row16)
    y_col = jnp.sum(y_pick * y_sum, axis=1, keepdims=True)
    modes_grad = modes_grad + jnp.where(lane16 == 32 + b_mode, y_col, 0.0)
    z_pick = flag(lax.rem(iota((16, 128), 1), RZ) == row16)
    z_sum = yz_sum * y_lane
    for n in range(2):
        z_col = jnp.sum(z_pick * jnp.sum(z_sum[n * 32:(n + 1) * 32], axis=0, keepdims=True), axis=1, keepdims=True)
        modes_grad = modes_grad + jnp.where(lane16 == 64 + 2 * z + n, z_col, 0.0)
    f_out[...] = modes_grad
    exchange(X_F_Z, lambda o: f_out, fz_in, z, along_z, at_z)

    receive(X_G_SPLIT, 0, gs_in)
    gz_out[...] = g_out[half] + gs_in[...]
    exchange(X_G_Z, lambda o: gz_out, gz_in, z, along_z, at_z)

    arrive(X_D_Z, d_in, along_z)
    taps = dot(d_in[...].reshape(256, 384), z_parts, TN)
    taps = (taps[:, :128] + taps[:, 128:]).astype(BF)
    get_rows9.wait()
    dy_out[...] = dot(rows9[...], taps).astype(BF).reshape(16, 32, 128)
    exchange(X_D_XY, lambda o: dy_out.at[o], dy_in, xy, along_xy, at_xy)

    get_swapt.wait()
    arrive(X_C_Z, c_in, along_z)
    cy_out[...] = dot(swapt[...], c_in[...].reshape(128, 128)).astype(BF).reshape(8, 16, 128)
    exchange(X_C_XY, lambda o: cy_out.at[lax.rem(o, 8)], cp_in.at[half], xy, along_xy, at_xy)

    arrive(X_F_Z, fz_in, along_z)
    fx_out[...] = jnp.sum(fz_in[...], axis=0)
    exchange(X_F_X, lambda o: fx_out, fx_in, x4, along_x, at_x)
    arrive(X_G_Z, gz_in, along_z)
    gx_out[...] = jnp.sum(gz_in[...], axis=0)
    exchange(X_G_X, lambda o: gx_out, gx_in, x4, along_x, at_x)
    arrive(X_F_X, fx_in, along_x)
    fy_out[...] = jnp.sum(fx_in[...], axis=0)
    exchange(X_F_Y, lambda o: fy_out, fy_in, y, along_y, at_y)
    arrive(X_G_X, gx_in, along_x)
    gy_out[...] = jnp.sum(gx_in[...], axis=0)
    exchange(X_G_Y, lambda o: gy_out, gy_in, y, along_y, at_y)

    arrive(X_C_XY, cp_in.at[half], along_xy)
    send(X_C_CORE, 0, 0, cp_in.at[half], cp_in.at[half], other_core)
    arrive(X_D_XY, dy_in, along_xy)
    theirs = pl.ds(pl.multiple_of((1 - half) * 16, 16), 16)
    ours = pl.ds(pl.multiple_of(half * 16, 16), 16)
    send(X_D_CORE, 0, 0, dy_in.at[:, theirs], dc_in, other_core)

    def deepen(group, modes_of):
        deep = dot(modes_of.reshape(128, 128), zblock[...], TN)
        for i in range(4):
            pair = [deep[:, (2 * i + h) * 128:(2 * i + h + 1) * 128].reshape(16, 8, 128) for h in range(2)]
            rows = pl.ds(pl.multiple_of(group * 64 + i * 16, 16), 16)
            zspec[:, rows, :] = jnp.concatenate(pair, axis=1).astype(BF)

    get_zblock.wait()
    for h in range(2):
        deepen(h * 2 + half, cp_in[half, h * 8:(h + 1) * 8])
    arrive(X_F_Y, fy_in, along_y)
    fc_out[...] = jnp.sum(fy_in[...], axis=0)
    send(X_F_CORE, 0, 0, fc_out, fc_in, other_core)
    arrive(X_G_Y, gy_in, along_y)
    gc_out[...] = jnp.sum(gy_in[...], axis=0)
    send(X_G_CORE, 0, 0, gc_out, gc_in, other_core)
    receive(X_C_CORE, 0, cp_in.at[1 - half])
    for h in range(2):
        deepen(h * 2 + 1 - half, cp_in[1 - half, h * 8:(h + 1) * 8])
    get_bwd.wait()
    for plane in range(2):
        for i in range(8):
            lines = dot(bwd[...], zspec[plane * 8 + i])
            out_features[i * 8:(i + 1) * 8, plane] = lines.reshape(8, 32, 128).astype(BF)

    get_widen.wait()
    receive(X_D_CORE, 0, dc_in)
    mine = dy_in[:, ours].reshape(256, 128)
    far = dc_in[...].reshape(256, 128)
    y_taps = y_taps.reshape(2, 2, 8, 128)
    y_mine = jnp.where(half == 0, y_taps[:, 0], y_taps[:, 1]).reshape(16, 1, 128)
    y_far = jnp.where(half == 0, y_taps[:, 1], y_taps[:, 0]).reshape(16, 1, 128)
    for r in range(RX):
        wide = widen[:, r * 128:(r + 1) * 128]
        total = dot(mine, wide).reshape(16, 16, 128) * y_mine + dot(far, wide).reshape(16, 16, 128) * y_far
        out_core[:, r * 128:(r + 1) * 128] = jnp.sum(total, axis=0)[:9]

    receive(X_F_CORE, 0, fc_in)
    out_modes[...] = fc_out[...] + fc_in[...]
    receive(X_G_CORE, 0, gc_in)
    for which, sums in ((half, gc_out[...]), (1 - half, gc_in[...])):
        out_pair[which] = jnp.concatenate([sums[:, :C], sums[:, C:]], axis=0)
    for copy in sends:
        copy.wait_send()


def write_out(planes, core_rows, pair, modes, features, core, g_in, g_out, g_x, g_y, g_z, x_v, y_v, z_v, sem):
    copies = [pltpu.make_async_copy(planes.at[i * 32:(i + 1) * 32], features.at[i * 32:(i + 1) * 32], sem.at[i]) for i in range(2)]
    copies.append(pltpu.make_async_copy(core_rows, core, sem.at[2]))
    copies.append(pltpu.make_async_copy(pair.at[0], g_in, sem.at[3]))
    copies.append(pltpu.make_async_copy(pair.at[1], g_out, sem.at[4]))
    for copy in copies:
        copy.start()
    x_v[...] = modes[:, 0:32]
    y_v[...] = modes[:, 32:64]
    z_v[...] = modes[0:8, 64:80]
    for i, (src, dst) in enumerate(((x_v, g_x), (y_v, g_y), (z_v, g_z))):
        copies.append(pltpu.make_async_copy(src, dst, sem.at[5 + i]))
        copies[-1].start()
    for copy in copies:
        copy.wait()


def shards(features, cotangent, tucker_core, in_factor, out_factor, x_factor, y_factor, z_factor):
    tables = [jnp.asarray(m) for m in constants()]
    hbm = pl.BlockSpec(memory_space=pltpu.HBM)
    vmem = pl.BlockSpec(memory_space=pltpu.VMEM)
    buffers = [
        ((2, 64, 2, 32, 128), BF), ((2304, 2048), BF), ((48, 64), F32), ((48, 64), F32), ((16, 32), F32),
        ((16, 32), F32), ((8, 16), F32),
        ((256, 256), BF), ((256, 256), BF), ((32, 128), BF), ((128, 1024), BF), ((2, 128, 128), BF),
        ((256, 128), BF), ((128, 256), BF), ((128, 128), BF), ((512, 384), BF), ((128, 2048), BF),
        ((32, 256, 128), BF), ((4, 8, 16, 256), BF), ((2, 8, 16, 256), BF), ((16, 16, 256), BF), ((16, 16, 256), BF),
        ((8, 16, 256), BF), ((8, 16, 256), BF),
        ((64, 2048), BF), ((2304, 64), F32), ((8, 384, 64), BF), ((8, 32, 384), BF), ((8, 32, 384), BF),
        ((48, 48, 64), F32), ((8, 16, 128), BF), ((8, 16, 128), BF),
        ((2, 24, 128), F32), ((24, 128), F32), ((24, 128), F32), ((8, 24, 128), F32), ((24, 128), F32),
        ((4, 24, 128), F32), ((24, 128), F32), ((4, 24, 128), F32), ((24, 128), F32), ((24, 128), F32),
        ((16, 128), F32), ((8, 16, 128), F32), ((16, 128), F32), ((4, 16, 128), F32), ((16, 128), F32),
        ((4, 16, 128), F32), ((16, 128), F32), ((16, 128), F32),
        ((16, 32, 128), BF), ((16, 32, 128), BF), ((16, 16, 128), BF), ((8, 16, 128), BF), ((2, 16, 16, 128), BF),
        ((16, 256, 128), BF),
    ]
    factors = (in_factor, out_factor, x_factor, y_factor, z_factor)
    operands = [features, cotangent, tucker_core] + [a.T for a in factors] + tables
    results = pl.pallas_call(
        kernel,
        out_shape=(
            pltpu.VMEM((C, 2, 32, NZ), BF),
            pltpu.VMEM((9, 2048), F32),
            pltpu.VMEM((2, RIN, C), F32),
            pltpu.VMEM((16, 128), F32),
        ),
        in_specs=[hbm] * (8 + len(tables)),
        out_specs=(vmem, vmem, vmem, vmem),
        scratch_shapes=[pltpu.VMEM(shape, dtype) for shape, dtype in buffers] + [
            pltpu.SemaphoreType.DMA((28,)),
            pltpu.SemaphoreType.DMA((18, 16)),
            pltpu.SemaphoreType.DMA((18, 16)),
        ],
        compiler_params=pltpu.CompilerParams(
            collective_id=0, has_side_effects=True, vmem_limit_bytes=32 * 1024 * 1024
        ),
    )(*[pltpu.with_memory_space_constraint(a, pltpu.HBM) for a in operands])
    outs = pl.pallas_call(
        write_out,
        out_shape=(
            jax.ShapeDtypeStruct((C, 2, 32, NZ), BF),
            jax.ShapeDtypeStruct((9, 2048), F32),
            jax.ShapeDtypeStruct((RIN, C), F32),
            jax.ShapeDtypeStruct((ROUT, C), F32),
            jax.ShapeDtypeStruct((RX, KX), F32),
            jax.ShapeDtypeStruct((RY, KY), F32),
            jax.ShapeDtypeStruct((RZ, KZ), F32),
        ),
        in_specs=[vmem] * 4,
        out_specs=[hbm] * 7,
        scratch_shapes=[
            pltpu.VMEM((RX, KX), F32), pltpu.VMEM((RY, KY), F32), pltpu.VMEM((RZ, KZ), F32),
            pltpu.SemaphoreType.DMA((8,)),
        ],
    )(*[pltpu.with_memory_space_constraint(a, pltpu.VMEM) for a in results])
    return outs[0], outs[1], outs[2].T, outs[3].T, outs[4].T, outs[5].T, outs[6].T


def solution(mesh):
    placed = (P(None, "px", "py", None), P(None, "px", "py", None), P(), P(), P(), P(), P(), P())
    return jax.shard_map(
        shards,
        mesh=mesh,
        in_specs=placed,
        out_specs=(P(None, "px", "py", None), P(("px", "py"), None), P(), P(), P(), P(), P()),
        check_vma=False,
    )
```

```python
import math

import jax
import jax.numpy as jnp
import numpy as np
from jax import lax
from jax.experimental import pallas as pl
from jax.experimental.pallas import tpu as pltpu
from jax.sharding import PartitionSpec as P

NX = 128
NY = 128
NZ = 128
KX = 32
KY = 32
KZ = 16
RIN = 48
ROUT = 48
RX = 16
RY = 16
RZ = 8
C = 64

BF = jnp.bfloat16
F32 = jnp.float32
MESH = pl.DeviceIdType.MESH
EXACT = lax.Precision.HIGHEST
NN = (((1,), (0,)), ((), ()))
NT = (((1,), (1,)), ((), ()))
TN = (((0,), (0,)), ((), ()))


def table(count, length):
    half = count // 2
    rows = np.arange(count)[:, None]
    cols = np.arange(length)[None, :]
    freq = np.where(rows < half, rows, rows - half + 1)
    angle = (freq * cols % length) * (2.0 * math.pi / length)
    values = np.where(rows < half, np.cos(angle), np.sin(angle)) * math.sqrt(2.0 / length)
    return values.astype(np.float32)


def two_parts(values):
    high = values.astype(jnp.bfloat16)
    low = (values - high.astype(np.float32)).astype(jnp.bfloat16)
    return high, low


def constants():
    ex, ey, ez = table(KX, NX), table(KY, NY), table(KZ, NZ)
    eye8 = np.eye(8, dtype=np.float32)
    strips = ey.reshape(KY, 4, 32).transpose(1, 0, 2)
    fwd = np.einsum("pjy,cd->pjcdy", strips, eye8).reshape(4, 256, 256)
    bwd = np.ascontiguousarray(fwd.transpose(0, 2, 1))
    z_high, z_low = two_parts(ez)
    z_rows = np.concatenate([z_high, z_low], 0)
    z_block = np.einsum("kz,ij->ikjz", z_high.astype(np.float32), eye8).reshape(128, 1024)
    planes = ex.reshape(KX, 2, 8, 4, 2)
    eye2 = np.eye(2, dtype=np.float32)
    gather = np.einsum("ayzxp,mn->pmaznyx", planes, eye2).reshape(2, 64, 128)
    gather = np.concatenate(two_parts(gather), 1)
    spread = np.einsum("ayzxp,mn->znyxpma", planes, eye2).reshape(128, 128)
    spread = np.concatenate(two_parts(spread), 0)
    swap = np.zeros((8, 2, 8, 8, 16), np.float32)
    for z in range(8):
        for n in range(2):
            for m in range(8):
                swap[z, n, m, m, 2 * z + n] = 1.0
    swap = swap.reshape(128, 128)
    swap_add = np.concatenate([swap, swap], 1)
    rows9 = np.zeros((2, 8, 2, 16, 2, 192), np.float32)
    for h in range(2):
        for m in range(8):
            for c in range(2):
                for q in range(9):
                    rows9[h, m, c, q, m // 4, (m % 4) * 36 + (h * 2 + c) * 9 + q] = 1.0
    widen = np.zeros((RX, RZ, RX, RY, RZ), np.float32)
    for r in range(RX):
        for t in range(RZ):
            widen[r, t, r, :, t] = 1.0
    mats = (
        fwd, bwd, z_rows, z_block, gather, spread, swap_add, np.ascontiguousarray(swap.T),
        rows9.reshape(512, 384), widen.reshape(128, 2048),
    )
    return [np.asarray(m).astype(jnp.bfloat16) for m in mats]


(
    X_A_CORE, X_A_XY, X_A_Z, X_D_Z, X_C_Z, X_D_XY, X_C_XY, X_D_CORE, X_C_CORE,
    X_G_SPLIT, X_G_Z, X_G_XY, X_G_CORE,
) = range(13)


def iota(shape, dim):
    return lax.broadcasted_iota(jnp.int32, shape, dim)


def flag(mask):
    return jnp.where(mask, 1.0, 0.0).astype(F32)


def dot(a, b, dims=NN, precision=None):
    return lax.dot_general(a, b, dims, precision=precision, preferred_element_type=F32)


def kernel(
    feat, cot, core, fin, fout, fx, fy, fz,
    k_fwd, k_bwd, k_zrows, k_zblock, k_gather, k_spread, k_swap, k_swapt, k_rows9, k_widen,
    out_features, out_core, out_pair, out_modes,
    field, core_v, fin_v, fout_v, fx_v, fy_v, fz_v,
    fwd, bwd, zrows, zblock, gather, spread, swap, swapt, rows9, widen,
    yspec, part, core_in, a_out, a_in, az_out, az_in,
    modes, uvt, uvp, d_out, d_in, w_all, c_out, c_in,
    g_out, gs_in, gz_out, gz_in, gx_out, gx_in, gc_out, gc_in,
    dy_out, dy_in, dc_in, cy_out, cp_in,
    zspec, local_sem, send_sem, recv_sem,
):
    px = lax.axis_index("px")
    py = lax.axis_index("py")
    x4 = lax.rem(px, 4)
    z = lax.rem(px // 4, 8)
    y_lo = px // 32
    yx = y_lo * 4 + x4
    y_hi = py // 2
    half = lax.rem(py, 2)
    y = y_hi * 2 + y_lo
    xy = y * 4 + x4
    other_core = (px, y_hi * 2 + 1 - half)

    def at_z(other):
        return (y_lo * 32 + other * 4 + x4, py)

    def at_xy(other):
        there = lax.rem(other, 8)
        return (there // 4 * 32 + z * 4 + lax.rem(there, 4), other // 8 * 2 + half)

    along_z = [lax.rem(z + d, 8) for d in (4, 3, 5, 2, 6, 1, 7)]
    along_xy = [
        lax.rem(y + dy, 4) * 4 + lax.rem(x4 + dx, 4)
        for dy, dx in (
            (2, 2), (2, 1), (2, 3), (1, 2), (3, 2), (2, 0), (0, 2), (1, 1),
            (1, 3), (3, 1), (3, 3), (1, 0), (3, 0), (0, 1), (0, 3),
        )
    ]

    loads = []

    def load(src, dst):
        copy = pltpu.make_async_copy(src, dst, local_sem.at[len(loads)])
        copy.start()
        loads.append(copy)
        return copy

    get_fwd = load(k_fwd.at[py], fwd)
    get_field = [
        [load(src.at[i * 16:(i + 1) * 16], field.at[f, i * 16:(i + 1) * 16]) for f, src in enumerate((feat, cot))]
        for i in range(4)
    ]

    barrier = pltpu.get_barrier_semaphore()
    for other in along_z:
        pl.semaphore_signal(barrier, inc=1, device_id=at_z(other), device_id_type=MESH)
    for other in along_xy:
        pl.semaphore_signal(barrier, inc=1, device_id=at_xy(other), device_id_type=MESH)
    pl.semaphore_signal(barrier, inc=1, device_id=other_core, device_id_type=MESH)

    get_zrows = load(k_zrows, zrows)
    get_small = [load(s, d) for s, d in ((fin, fin_v), (fout, fout_v), (fx, fx_v), (fy, fy_v), (fz, fz_v))]
    get_swap = load(k_swap, swap)
    get_gather = load(k_gather, gather)
    get_core = load(core, core_v)
    get_spread = load(k_spread, spread)
    get_rows9 = load(k_rows9, rows9)
    get_swapt = load(k_swapt, swapt)
    get_zblock = load(k_zblock, zblock)
    get_bwd = load(k_bwd.at[py], bwd)
    get_widen = load(k_widen, widen)

    sent = []

    def descriptor(number, src, dst, device):
        return pltpu.make_async_remote_copy(
            src_ref=src, dst_ref=dst, send_sem=send_sem.at[number], recv_sem=recv_sem.at[number],
            device_id=device, device_id_type=MESH,
        )

    def swap_cores(number, src, dst):
        copy = descriptor(number, src, dst, other_core)
        copy.start()
        sent.append(copy)
        return copy

    def exchange(number, src_of, into, mine, others, device_of):
        for other in others:
            descriptor(number, src_of(other), into.at[mine], device_of(other)).start()
        into[mine] = src_of(mine)[...]
        blocks = into.at[0:len(others)]
        whole = descriptor(number, blocks, blocks, other_core)
        sent.append(whole)
        return whole

    get_fwd.wait()
    for i in range(4):
        for f in range(2):
            get_field[i][f].wait()

            def lines(plane, carry, i=i, f=f):
                pair = []
                for h in range(2):
                    c = i * 16 + h * 8
                    block = field[f, c:c + 8, plane].reshape(256, NZ)
                    pair.append(dot(fwd[...], block).reshape(KY, 8, NZ))
                rows = pl.ds(pl.multiple_of(plane * 128 + f * 64 + i * 16, 16), 16)
                yspec[:, rows, :] = jnp.concatenate(pair, axis=1).astype(BF)
                return carry

            lax.fori_loop(0, 2, lines, 0, unroll=True)
    get_zrows.wait()

    def depth(c, h):
        def one(i, carry):
            both = dot(zrows[...], yspec[(h * 2 + c) * 8 + i], NT)
            part[c, h * 8 + i] = (both[:KZ] + both[KZ:]).astype(BF)
            return carry

        lax.fori_loop(0, 8, one, 0, unroll=4)

    for h in range(2):
        depth(1 - half, h)
    pl.semaphore_wait(barrier, 23)
    a_core = swap_cores(X_A_CORE, part.at[1 - half], core_in)
    for h in range(2):
        depth(half, h)

    a_core.wait_recv()
    a_out[...] = (part[half].astype(F32) + core_in[...].astype(F32)).astype(BF)
    a_xy = exchange(X_A_XY, lambda o: a_out.at[o], a_in, xy, along_xy, at_xy)

    for copy in get_small:
        copy.wait()
    fin_t = dot(fin_v[...], flag(lax.rem(iota((C, 128), 1), C) == iota((C, 128), 0)), NN, EXACT)
    fout_t = fout_v[...]
    b_mode = py * 8 + yx
    y_rows = dot(flag(iota((64, KY), 1) == b_mode), fy_v[...], NT, EXACT)
    z_rows = dot(flag(iota((64, KZ), 1) == 2 * z + iota((64, KZ), 0) // 32), fz_v[...], NT, EXACT)
    y_wide = flag(iota((RY, 128), 1) // RZ == iota((RY, 128), 0))
    z_wide = flag(lax.rem(iota((RZ, 128), 1), RZ) == iota((RZ, 128), 0))
    y_lane = dot(y_rows, y_wide, NN, EXACT)
    z_lane = dot(z_rows, z_wide, NN, EXACT)
    yz_lane = y_lane * z_lane
    x_rep = dot(flag(iota((64, KX), 1) == lax.rem(iota((64, KX), 0), KX)), fx_v[...], NT, EXACT)
    for r in range(RX):
        modes[:, r * 128:(r + 1) * 128] = (x_rep[:, r:r + 1] * yz_lane).astype(BF)
    x_cols = dot(fx_v[...], flag(lax.rem(iota((KX, 64), 1), KX) == iota((KX, 64), 0)), NN, EXACT)
    x_cols = jnp.concatenate([x_cols, x_cols], axis=0)
    x_cols = jnp.where(iota((32, 64), 0) // RX == iota((32, 64), 1) // KX, x_cols, 0.0)
    x_high = x_cols.astype(BF)
    x_parts = jnp.concatenate([x_cols, x_cols - x_high.astype(F32)], axis=0).astype(BF)
    z_taps = dot(flag(iota((256, KZ), 0) // RX == iota((256, KZ), 1)), fz_v[...], NT, EXACT)
    z_taps = dot(z_taps, z_wide, NN, EXACT)
    z_taps = jnp.where(lax.rem(iota((256, 128), 0), RX) == iota((256, 128), 1) // RZ, z_taps, 0.0)
    z_high = z_taps.astype(BF)
    z_parts = jnp.concatenate([z_taps, z_taps - z_high.astype(F32)], axis=1).astype(BF)
    y_taps = dot(fy_v[...], y_wide, TN, EXACT)
    for block in range(8):
        for m in range(2):
            uvp[block, m * 192 + 144:(m + 1) * 192, :] = jnp.zeros((48, 64), BF)

    get_swap.wait()
    a_xy.wait_recv()
    az_out[...] = dot(swap[...], a_in[...].reshape(256, 256)).astype(BF).reshape(8, 16, 256)
    a_z = exchange(X_A_Z, lambda o: az_out.at[o], az_in, z, along_z, at_z)

    get_core.wait()
    for g in range(8):
        w_all[g * 6:(g + 1) * 6] = dot(core_v[g * 288:(g + 1) * 288, :], modes[...], NT).reshape(6, 48, 64)

    get_gather.wait()
    a_z.wait_recv()
    slabs = az_in[...].reshape(128, 256)
    both = dot(gather[0], slabs[:, :128]) + dot(gather[1], slabs[:, 128:])
    spec = both[:64] + both[64:]
    spec_t = spec.T

    u_t = dot(fin_t[:, :C], spec_t[:C], NN, EXACT)
    v_t = dot(fout_t, spec_t[C:], NN, EXACT)
    for g in range(16):
        rows = u_t[g * 3:(g + 1) * 3][:, None, :] * v_t[None, :, :]
        rows = rows.reshape(144, 64)
        uvt[g * 144:(g + 1) * 144, :] = rows
        uvp[g % 8, (g // 8) * 192:(g // 8) * 192 + 144, :] = rows.astype(BF)
    for g in range(8):
        flow = dot(x_parts, uvp[g], NT)
        d_out[g] = (flow[:32] + flow[32:]).astype(BF)
    d_z = exchange(X_D_Z, lambda o: d_out.at[o], d_in, z, along_z, at_z)

    weight = w_all[...]
    h_t = jnp.sum(weight * v_t[None, :, :], axis=1)
    pulled = dot(h_t, fin_t, TN, EXACT)
    lane = iota((64, 128), 1)
    pulled = jnp.concatenate(
        [jnp.where(lane < C, pulled, 0.0), jnp.where(lane >= C, pulled, 0.0)], axis=0
    ).astype(BF)
    get_spread.wait()
    synth = dot(spread[...], pulled)
    c_out[...] = (synth[:128] + synth[128:]).astype(BF).reshape(8, 16, 128)
    c_z = exchange(X_C_Z, lambda o: c_out.at[o], c_in, z, along_z, at_z)

    g_t = jnp.sum(weight * u_t[:, None, :], axis=0)
    for f, ranks in enumerate((h_t, g_t)):
        grad = dot(ranks, spec[:, f * C:(f + 1) * C], NN, EXACT)
        g_out[f, :24] = jnp.concatenate([grad[:24], grad[24:]], axis=1)

    uv = uvt[...].T.astype(BF)
    x_sum = jnp.zeros((64, 128), F32)
    yz_sum = jnp.zeros((64, 128), F32)
    for g in range(8):
        flow = dot(uv, core_v[:, g * 256:(g + 1) * 256])
        for h in range(2):
            r = g * 2 + h
            piece = flow[:, h * 128:(h + 1) * 128]
            x_sum = x_sum + jnp.where(lane == r, jnp.sum(piece * yz_lane, axis=1, keepdims=True), 0.0)
            yz_sum = yz_sum + piece * x_rep[:, r:r + 1]
    row16 = iota((16, 128), 0)
    lane16 = iota((16, 128), 1)
    modes_grad = dot(
        flag(iota((16, 128), 0) == iota((16, 128), 1)), x_sum[:32] + x_sum[32:], NT, EXACT
    )
    modes_grad = jnp.concatenate([modes_grad, jnp.zeros((16, 96), F32)], axis=1)
    y_sum = jnp.sum(yz_sum * z_lane, axis=0, keepdims=True)
    y_pick = flag(iota((16, 128), 1) // RZ == row16)
    y_col = jnp.sum(y_pick * y_sum, axis=1, keepdims=True)
    modes_grad = modes_grad + jnp.where(lane16 == 32 + b_mode, y_col, 0.0)
    z_pick = flag(lax.rem(iota((16, 128), 1), RZ) == row16)
    z_sum = yz_sum * y_lane
    for n in range(2):
        z_col = jnp.sum(z_pick * jnp.sum(z_sum[n * 32:(n + 1) * 32], axis=0, keepdims=True), axis=1, keepdims=True)
        modes_grad = modes_grad + jnp.where(lane16 == 64 + 2 * z + n, z_col, 0.0)
    for f in range(2):
        g_out[f, 24:] = modes_grad[f * 8:(f + 1) * 8]
    g_split = swap_cores(X_G_SPLIT, g_out.at[1 - half], gs_in)
    g_split.wait_recv()
    gz_out[...] = (g_out[half] + gs_in[...]).astype(BF)
    g_z = exchange(X_G_Z, lambda o: gz_out, gz_in, z, along_z, at_z)

    d_z.wait_recv()
    taps = dot(d_in[...].reshape(256, 384), z_parts, TN)
    taps = (taps[:, :128] + taps[:, 128:]).astype(BF)
    get_rows9.wait()
    dy_out[...] = dot(rows9[...], taps).astype(BF).reshape(16, 32, 128)
    d_xy = exchange(X_D_XY, lambda o: dy_out.at[o], dy_in, xy, along_xy, at_xy)

    get_swapt.wait()
    c_z.wait_recv()
    cy_out[...] = dot(swapt[...], c_in[...].reshape(128, 128)).astype(BF).reshape(8, 16, 128)
    c_xy = exchange(X_C_XY, lambda o: cy_out.at[lax.rem(o, 8)], cp_in.at[half], xy, along_xy, at_xy)

    g_z.wait_recv()
    gx_out[...] = jnp.sum(gz_in[...].astype(F32), axis=0).astype(BF)
    g_xy = exchange(X_G_XY, lambda o: gx_out, gx_in, xy, along_xy, at_xy)

    c_xy.wait_recv()
    c_core = swap_cores(X_C_CORE, cp_in.at[half], cp_in.at[half])
    d_xy.wait_recv()
    theirs = pl.ds(pl.multiple_of((1 - half) * 16, 16), 16)
    ours = pl.ds(pl.multiple_of(half * 16, 16), 16)
    d_core = swap_cores(X_D_CORE, dy_in.at[:, theirs], dc_in)

    def deepen(group, modes_of):
        deep = dot(modes_of.reshape(128, 128), zblock[...], TN)
        for i in range(4):
            pair = [deep[:, (2 * i + h) * 128:(2 * i + h + 1) * 128].reshape(16, 8, 128) for h in range(2)]
            rows = pl.ds(pl.multiple_of(group * 64 + i * 16, 16), 16)
            zspec[:, rows, :] = jnp.concatenate(pair, axis=1).astype(BF)

    get_zblock.wait()
    for h in range(2):
        deepen(h * 2 + half, cp_in[half, h * 8:(h + 1) * 8])
    c_core.wait_recv()
    for h in range(2):
        deepen(h * 2 + 1 - half, cp_in[1 - half, h * 8:(h + 1) * 8])
    get_bwd.wait()
    for plane in range(2):
        for i in range(8):
            lines = dot(bwd[...], zspec[plane * 8 + i])
            out_features[i * 8:(i + 1) * 8, plane] = lines.reshape(8, 32, 128).astype(BF)

    get_widen.wait()
    d_core.wait_recv()
    mine = dy_in[:, ours].reshape(256, 128)
    far = dc_in[...].reshape(256, 128)
    y_taps = y_taps.reshape(2, 2, 8, 128)
    y_mine = jnp.where(half == 0, y_taps[:, 0], y_taps[:, 1]).reshape(16, 1, 128)
    y_far = jnp.where(half == 0, y_taps[:, 1], y_taps[:, 0]).reshape(16, 1, 128)
    for r in range(RX):
        wide = widen[:, r * 128:(r + 1) * 128]
        total = dot(mine, wide).reshape(16, 16, 128) * y_mine + dot(far, wide).reshape(16, 16, 128) * y_far
        out_core[:, r * 128:(r + 1) * 128] = jnp.sum(total, axis=0)[:9]

    g_xy.wait_recv()
    gc_out[...] = jnp.sum(gx_in[...].astype(F32), axis=0)
    g_core = swap_cores(X_G_CORE, gc_out, gc_in)
    g_core.wait_recv()
    for which, sums in ((half, gc_out[...]), (1 - half, gc_in[...])):
        out_pair[which] = jnp.concatenate([sums[:24, :C], sums[:24, C:]], axis=0)
        out_modes[which] = sums[24:]
    for copy in sent:
        copy.wait_send()


def write_out(planes, core_rows, pair, modes, features, core, g_in, g_out, g_x, g_y, g_z, x_v, y_v, z_v, sem):
    copies = [pltpu.make_async_copy(planes.at[i * 32:(i + 1) * 32], features.at[i * 32:(i + 1) * 32], sem.at[i]) for i in range(2)]
    copies.append(pltpu.make_async_copy(core_rows, core, sem.at[2]))
    copies.append(pltpu.make_async_copy(pair.at[0], g_in, sem.at[3]))
    copies.append(pltpu.make_async_copy(pair.at[1], g_out, sem.at[4]))
    for copy in copies:
        copy.start()
    x_v[...] = modes[...].reshape(16, 128)[:, 0:32]
    y_v[...] = modes[...].reshape(16, 128)[:, 32:64]
    z_v[...] = modes[0, :, 64:80]
    for i, (src, dst) in enumerate(((x_v, g_x), (y_v, g_y), (z_v, g_z))):
        copies.append(pltpu.make_async_copy(src, dst, sem.at[5 + i]))
        copies[-1].start()
    for copy in copies:
        copy.wait()


def shards(features, cotangent, tucker_core, in_factor, out_factor, x_factor, y_factor, z_factor):
    tables = [jnp.asarray(m) for m in constants()]
    hbm = pl.BlockSpec(memory_space=pltpu.HBM)
    vmem = pl.BlockSpec(memory_space=pltpu.VMEM)
    buffers = [
        ((2, 64, 2, 32, 128), BF), ((2304, 2048), BF), ((48, 64), F32), ((48, 64), F32), ((16, 32), F32),
        ((16, 32), F32), ((8, 16), F32),
        ((256, 256), BF), ((256, 256), BF), ((32, 128), BF), ((128, 1024), BF), ((2, 128, 128), BF),
        ((256, 128), BF), ((128, 256), BF), ((128, 128), BF), ((512, 384), BF), ((128, 2048), BF),
        ((32, 256, 128), BF), ((2, 16, 16, 256), BF), ((16, 16, 256), BF), ((16, 16, 256), BF), ((16, 16, 256), BF),
        ((8, 16, 256), BF), ((8, 16, 256), BF),
        ((64, 2048), BF), ((2304, 64), F32), ((8, 384, 64), BF), ((8, 32, 384), BF), ((8, 32, 384), BF),
        ((48, 48, 64), F32), ((8, 16, 128), BF), ((8, 16, 128), BF),
        ((2, 32, 128), F32), ((32, 128), F32), ((32, 128), BF), ((8, 32, 128), BF), ((32, 128), BF),
        ((16, 32, 128), BF), ((32, 128), F32), ((32, 128), F32),
        ((16, 32, 128), BF), ((16, 32, 128), BF), ((16, 16, 128), BF), ((8, 16, 128), BF), ((2, 16, 16, 128), BF),
        ((16, 256, 128), BF),
    ]
    factors = (in_factor, out_factor, x_factor, y_factor, z_factor)
    operands = [features, cotangent, tucker_core] + [a.T for a in factors] + tables
    results = pl.pallas_call(
        kernel,
        out_shape=(
            pltpu.VMEM((C, 2, 32, NZ), BF),
            pltpu.VMEM((9, 2048), F32),
            pltpu.VMEM((2, RIN, C), F32),
            pltpu.VMEM((2, 8, 128), F32),
        ),
        in_specs=[hbm] * (8 + len(tables)),
        out_specs=(vmem, vmem, vmem, vmem),
        scratch_shapes=[pltpu.VMEM(shape, dtype) for shape, dtype in buffers] + [
            pltpu.SemaphoreType.DMA((24,)),
            pltpu.SemaphoreType.DMA((13,)),
            pltpu.SemaphoreType.DMA((13,)),
        ],
        compiler_params=pltpu.CompilerParams(
            collective_id=0, has_side_effects=True, vmem_limit_bytes=32 * 1024 * 1024
        ),
    )(*[pltpu.with_memory_space_constraint(a, pltpu.HBM) for a in operands])
    outs = pl.pallas_call(
        write_out,
        out_shape=(
            jax.ShapeDtypeStruct((C, 2, 32, NZ), BF),
            jax.ShapeDtypeStruct((9, 2048), F32),
            jax.ShapeDtypeStruct((RIN, C), F32),
            jax.ShapeDtypeStruct((ROUT, C), F32),
            jax.ShapeDtypeStruct((RX, KX), F32),
            jax.ShapeDtypeStruct((RY, KY), F32),
            jax.ShapeDtypeStruct((RZ, KZ), F32),
        ),
        in_specs=[vmem] * 4,
        out_specs=[hbm] * 7,
        scratch_shapes=[
            pltpu.VMEM((RX, KX), F32), pltpu.VMEM((RY, KY), F32), pltpu.VMEM((RZ, KZ), F32),
            pltpu.SemaphoreType.DMA((8,)),
        ],
    )(*[pltpu.with_memory_space_constraint(a, pltpu.VMEM) for a in results])
    return outs[0], outs[1], outs[2].T, outs[3].T, outs[4].T, outs[5].T, outs[6].T


def solution(mesh):
    placed = (P(None, "px", "py", None), P(None, "px", "py", None), P(), P(), P(), P(), P(), P())
    return jax.shard_map(
        shards,
        mesh=mesh,
        in_specs=placed,
        out_specs=(P(None, "px", "py", None), P(("px", "py"), None), P(), P(), P(), P(), P()),
        check_vma=False,
    )
```

```python
import math

import jax
import jax.numpy as jnp
import numpy as np
from jax import lax
from jax.experimental import pallas as pl
from jax.experimental.pallas import tpu as pltpu
from jax.sharding import PartitionSpec as P

NX = 128
NY = 128
NZ = 128
KX = 32
KY = 32
KZ = 16
RIN = 48
ROUT = 48
RX = 16
RY = 16
RZ = 8
C = 64

BF = jnp.bfloat16
F32 = jnp.float32
MESH = pl.DeviceIdType.MESH
EXACT = lax.Precision.HIGHEST
NN = (((1,), (0,)), ((), ()))
NT = (((1,), (1,)), ((), ()))
TN = (((0,), (0,)), ((), ()))


def table(count, length):
    half = count // 2
    rows = np.arange(count)[:, None]
    cols = np.arange(length)[None, :]
    freq = np.where(rows < half, rows, rows - half + 1)
    angle = (freq * cols % length) * (2.0 * math.pi / length)
    values = np.where(rows < half, np.cos(angle), np.sin(angle)) * math.sqrt(2.0 / length)
    return values.astype(np.float32)


def two_parts(values):
    high = values.astype(jnp.bfloat16)
    low = (values - high.astype(np.float32)).astype(jnp.bfloat16)
    return high, low


def constants():
    ex, ey, ez = table(KX, NX), table(KY, NY), table(KZ, NZ)
    eye8 = np.eye(8, dtype=np.float32)
    strips = ey.reshape(KY, 4, 32).transpose(1, 0, 2)
    fwd = np.einsum("pjy,cd->pjcdy", strips, eye8).reshape(4, 256, 256)
    bwd = np.ascontiguousarray(fwd.transpose(0, 2, 1))
    z_high, z_low = two_parts(ez)
    z_rows = np.concatenate([z_high, z_low], 0)
    z_block = np.einsum("kz,ij->ikjz", z_high.astype(np.float32), eye8).reshape(128, 1024)
    planes = ex.reshape(KX, 2, 8, 4, 2)
    eye2 = np.eye(2, dtype=np.float32)
    gather = np.einsum("ayzxp,mn->pmaznyx", planes, eye2).reshape(2, 64, 128)
    gather = np.concatenate(two_parts(gather), 1)
    spread = np.einsum("ayzxp,mn->znyxpma", planes, eye2).reshape(128, 128)
    spread = np.concatenate(two_parts(spread), 0)
    swap = np.zeros((8, 2, 8, 8, 16), np.float32)
    for z in range(8):
        for n in range(2):
            for m in range(8):
                swap[z, n, m, m, 2 * z + n] = 1.0
    swap = swap.reshape(128, 128)
    swap_add = np.concatenate([swap, swap], 1)
    rows9 = np.zeros((2, 8, 2, 16, 2, 192), np.float32)
    for h in range(2):
        for m in range(8):
            for c in range(2):
                for q in range(9):
                    rows9[h, m, c, q, m // 4, (m % 4) * 36 + (h * 2 + c) * 9 + q] = 1.0
    widen = np.zeros((RX, RZ, RX, RY, RZ), np.float32)
    for r in range(RX):
        for t in range(RZ):
            widen[r, t, r, :, t] = 1.0
    mats = (
        fwd, bwd, z_rows, z_block, gather, spread, swap_add, np.ascontiguousarray(swap.T),
        rows9.reshape(512, 384), widen.reshape(128, 2048),
    )
    return [np.asarray(m).astype(jnp.bfloat16) for m in mats]


(
    X_A_CORE, X_A_XY, X_A_Z, X_D_Z, X_C_Z, X_DC_XY, X_D_CORE, X_C_CORE,
    X_G_SPLIT, X_G_Z, X_G_XY, X_G_CORE,
) = range(12)


def iota(shape, dim):
    return lax.broadcasted_iota(jnp.int32, shape, dim)


def flag(mask):
    return jnp.where(mask, 1.0, 0.0).astype(F32)


def dot(a, b, dims=NN, precision=None):
    return lax.dot_general(a, b, dims, precision=precision, preferred_element_type=F32)


def kernel(
    feat, cot, core, fin, fout, fx, fy, fz,
    k_fwd, k_bwd, k_zrows, k_zblock, k_gather, k_spread, k_swap, k_swapt, k_rows9, k_widen,
    out_features, out_core, out_pair, out_modes,
    field, core_v, fin_v, fout_v, fx_v, fy_v, fz_v,
    fwd, bwd, zrows, zblock, gather, spread, swap, swapt, rows9, widen,
    yspec, part, core_in, a_out, a_in, az_out, az_in,
    modes, x_wide, uvt, uvp, d_out, d_in, w_all, c_out, c_in,
    g_out, gs_in, gz_out, gz_in, gx_out, gx_in, gc_out, gc_in,
    dc_out, dc_in, d_far, c_far,
    zspec, local_sem, send_sem, recv_sem,
):
    px = lax.axis_index("px")
    py = lax.axis_index("py")
    x4 = lax.rem(px, 4)
    z = lax.rem(px // 4, 8)
    y_lo = px // 32
    yx = y_lo * 4 + x4
    y_hi = py // 2
    half = lax.rem(py, 2)
    y = y_hi * 2 + y_lo
    xy = y * 4 + x4
    other_core = (px, y_hi * 2 + 1 - half)

    def at_z(other):
        return (y_lo * 32 + other * 4 + x4, py)

    def at_xy(other):
        there = lax.rem(other, 8)
        return (there // 4 * 32 + z * 4 + lax.rem(there, 4), other // 8 * 2 + half)

    along_z = [lax.rem(z + d, 8) for d in (4, 3, 5, 2, 6, 1, 7)]
    along_xy = [
        lax.rem(y + dy, 4) * 4 + lax.rem(x4 + dx, 4)
        for dy, dx in (
            (2, 2), (2, 1), (2, 3), (1, 2), (3, 2), (2, 0), (0, 2), (1, 1),
            (1, 3), (3, 1), (3, 3), (1, 0), (3, 0), (0, 1), (0, 3),
        )
    ]

    loads = []

    def load(src, dst):
        copy = pltpu.make_async_copy(src, dst, local_sem.at[len(loads)])
        copy.start()
        loads.append(copy)
        return copy

    get_fwd = load(k_fwd.at[py], fwd)
    get_field = [
        [load(src.at[i * 16:(i + 1) * 16], field.at[f, i * 16:(i + 1) * 16]) for f, src in enumerate((feat, cot))]
        for i in range(4)
    ]

    barrier = pltpu.get_barrier_semaphore()
    for other in along_z:
        pl.semaphore_signal(barrier, inc=1, device_id=at_z(other), device_id_type=MESH)
    for other in along_xy:
        pl.semaphore_signal(barrier, inc=1, device_id=at_xy(other), device_id_type=MESH)
    pl.semaphore_signal(barrier, inc=1, device_id=other_core, device_id_type=MESH)

    get_zrows = load(k_zrows, zrows)
    get_small = [load(s, d) for s, d in ((fin, fin_v), (fout, fout_v), (fx, fx_v), (fy, fy_v), (fz, fz_v))]
    get_swap = load(k_swap, swap)
    get_gather = load(k_gather, gather)
    get_core = load(core, core_v)
    get_spread = load(k_spread, spread)
    get_rows9 = load(k_rows9, rows9)
    get_swapt = load(k_swapt, swapt)
    get_zblock = load(k_zblock, zblock)
    get_bwd = load(k_bwd.at[py], bwd)
    get_widen = load(k_widen, widen)

    sent = []

    def descriptor(number, src, dst, device):
        return pltpu.make_async_remote_copy(
            src_ref=src, dst_ref=dst, send_sem=send_sem.at[number], recv_sem=recv_sem.at[number],
            device_id=device, device_id_type=MESH,
        )

    def swap_cores(number, src, dst):
        copy = descriptor(number, src, dst, other_core)
        copy.start()
        sent.append(copy)
        return copy

    def exchange(number, src_of, into, mine, others, device_of):
        for other in others:
            descriptor(number, src_of(other), into.at[mine], device_of(other)).start()
        into[mine] = src_of(mine)[...]
        blocks = into.at[0:len(others)]
        whole = descriptor(number, blocks, blocks, other_core)
        sent.append(whole)
        return whole

    get_fwd.wait()
    for i in range(4):
        for f in range(2):
            get_field[i][f].wait()

            def lines(plane, carry, i=i, f=f):
                pair = []
                for h in range(2):
                    c = i * 16 + h * 8
                    block = field[f, c:c + 8, plane].reshape(256, NZ)
                    pair.append(dot(fwd[...], block).reshape(KY, 8, NZ))
                rows = pl.ds(pl.multiple_of(plane * 128 + f * 64 + i * 16, 16), 16)
                yspec[:, rows, :] = jnp.concatenate(pair, axis=1).astype(BF)
                return carry

            lax.fori_loop(0, 2, lines, 0, unroll=True)
    get_zrows.wait()

    def depth(c, h):
        def one(i, carry):
            both = dot(zrows[...], yspec[(h * 2 + c) * 8 + i], NT)
            part[c, h * 8 + i] = both[:KZ] + both[KZ:]
            return carry

        lax.fori_loop(0, 8, one, 0, unroll=4)

    for h in range(2):
        depth(1 - half, h)
    pl.semaphore_wait(barrier, 23)
    a_core = swap_cores(X_A_CORE, part.at[1 - half], core_in)
    for h in range(2):
        depth(half, h)

    a_core.wait_recv()
    a_out[...] = (part[half] + core_in[...]).astype(BF)
    a_xy = exchange(X_A_XY, lambda o: a_out.at[o], a_in, xy, along_xy, at_xy)

    for copy in get_small:
        copy.wait()
    fin_t = dot(fin_v[...], flag(lax.rem(iota((C, 128), 1), C) == iota((C, 128), 0)), NN, EXACT)
    fout_t = fout_v[...]
    b_mode = py * 8 + yx
    y_rows = dot(flag(iota((64, KY), 1) == b_mode), fy_v[...], NT, EXACT)
    z_rows = dot(flag(iota((64, KZ), 1) == 2 * z + iota((64, KZ), 0) // 32), fz_v[...], NT, EXACT)
    y_wide = flag(iota((RY, 128), 1) // RZ == iota((RY, 128), 0))
    z_wide = flag(lax.rem(iota((RZ, 128), 1), RZ) == iota((RZ, 128), 0))
    y_lane = dot(y_rows, y_wide, NN, EXACT)
    z_lane = dot(z_rows, z_wide, NN, EXACT)
    yz_lane = y_lane * z_lane
    x_rep = dot(flag(iota((64, KX), 1) == lax.rem(iota((64, KX), 0), KX)), fx_v[...], NT, EXACT)
    for r in range(RX):
        x_wide[:, r * 128:(r + 1) * 128] = jnp.broadcast_to(x_rep[:, r:r + 1], (64, 128))
        column = x_wide[:, r * 128:(r + 1) * 128] * yz_lane
        high = column.astype(BF)
        modes[:64, r * 128:(r + 1) * 128] = high
        modes[64:, r * 128:(r + 1) * 128] = (column - high.astype(F32)).astype(BF)
    x_cols = dot(fx_v[...], flag(lax.rem(iota((KX, 64), 1), KX) == iota((KX, 64), 0)), NN, EXACT)
    x_cols = jnp.concatenate([x_cols, x_cols], axis=0)
    x_cols = jnp.where(iota((32, 64), 0) // RX == iota((32, 64), 1) // KX, x_cols, 0.0)
    x_high = x_cols.astype(BF)
    x_parts = jnp.concatenate([x_cols, x_cols - x_high.astype(F32)], axis=0).astype(BF)
    z_taps = dot(flag(iota((256, KZ), 0) // RX == iota((256, KZ), 1)), fz_v[...], NT, EXACT)
    z_taps = dot(z_taps, z_wide, NN, EXACT)
    z_taps = jnp.where(lax.rem(iota((256, 128), 0), RX) == iota((256, 128), 1) // RZ, z_taps, 0.0)
    z_high = z_taps.astype(BF)
    z_parts = jnp.concatenate([z_taps, z_taps - z_high.astype(F32)], axis=1).astype(BF)
    y_taps = dot(fy_v[...], y_wide, TN, EXACT)
    for block in range(8):
        for m in range(2):
            uvp[block, m * 192 + 144:(m + 1) * 192, :] = jnp.zeros((48, 64), BF)

    get_swap.wait()
    a_xy.wait_recv()
    az_out[...] = dot(swap[...], a_in[...].reshape(256, 256)).astype(BF).reshape(8, 16, 256)
    a_z = exchange(X_A_Z, lambda o: az_out.at[o], az_in, z, along_z, at_z)

    get_core.wait()
    for g in range(8):
        both = dot(core_v[g * 288:(g + 1) * 288, :], modes[...], NT)
        w_all[g * 6:(g + 1) * 6] = (both[:, :64] + both[:, 64:]).reshape(6, 48, 64)

    get_gather.wait()
    a_z.wait_recv()
    slabs = az_in[...].reshape(128, 256)
    both = dot(gather[0], slabs[:, :128]) + dot(gather[1], slabs[:, 128:])
    spec = both[:64] + both[64:]
    spec_t = spec.T

    u_t = dot(fin_t[:, :C], spec_t[:C], NN, EXACT)
    v_t = dot(fout_t, spec_t[C:], NN, EXACT)
    for g in range(16):
        rows = u_t[g * 3:(g + 1) * 3][:, None, :] * v_t[None, :, :]
        rows = rows.reshape(144, 64)
        uvt[g * 144:(g + 1) * 144, :] = rows
        uvp[g % 8, (g // 8) * 192:(g // 8) * 192 + 144, :] = rows.astype(BF)
    for g in range(8):
        flow = dot(x_parts, uvp[g], NT)
        d_out[g] = (flow[:32] + flow[32:]).astype(BF)
    d_z = exchange(X_D_Z, lambda o: d_out.at[o], d_in, z, along_z, at_z)

    weight = w_all[...]
    h_t = jnp.sum(weight * v_t[None, :, :], axis=1)
    pulled = dot(h_t, fin_t, TN, EXACT)
    lane = iota((64, 128), 1)
    pulled = jnp.concatenate(
        [jnp.where(lane < C, pulled, 0.0), jnp.where(lane >= C, pulled, 0.0)], axis=0
    ).astype(BF)
    get_spread.wait()
    synth = dot(spread[...], pulled)
    c_out[...] = (synth[:128] + synth[128:]).astype(BF).reshape(8, 16, 128)
    c_z = exchange(X_C_Z, lambda o: c_out.at[o], c_in, z, along_z, at_z)

    g_t = jnp.sum(weight * u_t[:, None, :], axis=0)
    for f, ranks in enumerate((h_t, g_t)):
        grad = dot(ranks, spec[:, f * C:(f + 1) * C], NN, EXACT)
        g_out[f, :24] = jnp.concatenate([grad[:24], grad[24:]], axis=1)

    uv = uvt[...].T.astype(BF)
    x_sum = jnp.zeros((64, 128), F32)
    yz_sum = jnp.zeros((64, 128), F32)
    for g in range(8):
        flow = dot(uv, core_v[:, g * 256:(g + 1) * 256])
        for h in range(2):
            r = g * 2 + h
            piece = flow[:, h * 128:(h + 1) * 128]
            x_sum = x_sum + jnp.where(lane == r, jnp.sum(piece * yz_lane, axis=1, keepdims=True), 0.0)
            yz_sum = yz_sum + piece * x_wide[:, r * 128:(r + 1) * 128]
    row16 = iota((16, 128), 0)
    lane16 = iota((16, 128), 1)
    modes_grad = dot(
        flag(iota((16, 128), 0) == iota((16, 128), 1)), x_sum[:32] + x_sum[32:], NT, EXACT
    )
    modes_grad = jnp.concatenate([modes_grad, jnp.zeros((16, 96), F32)], axis=1)
    y_sum = jnp.sum(yz_sum * z_lane, axis=0, keepdims=True)
    y_pick = flag(iota((16, 128), 1) // RZ == row16)
    y_col = jnp.sum(y_pick * y_sum, axis=1, keepdims=True)
    modes_grad = modes_grad + jnp.where(lane16 == 32 + b_mode, y_col, 0.0)
    z_pick = flag(lax.rem(iota((16, 128), 1), RZ) == row16)
    z_sum = yz_sum * y_lane
    for n in range(2):
        z_col = jnp.sum(z_pick * jnp.sum(z_sum[n * 32:(n + 1) * 32], axis=0, keepdims=True), axis=1, keepdims=True)
        modes_grad = modes_grad + jnp.where(lane16 == 64 + 2 * z + n, z_col, 0.0)
    for f in range(2):
        g_out[f, 24:] = modes_grad[f * 8:(f + 1) * 8]
    g_split = swap_cores(X_G_SPLIT, g_out.at[1 - half], gs_in)
    g_split.wait_recv()
    gz_out[...] = (g_out[half] + gs_in[...]).astype(BF)
    g_z = exchange(X_G_Z, lambda o: gz_out, gz_in, z, along_z, at_z)

    d_z.wait_recv()
    taps = dot(d_in[...].reshape(256, 384), z_parts, TN)
    taps = (taps[:, :128] + taps[:, 128:]).astype(BF)
    get_rows9.wait()
    dc_out[:, :32] = dot(rows9[...], taps).astype(BF).reshape(16, 32, 128)

    get_swapt.wait()
    c_z.wait_recv()
    planes = dot(swapt[...], c_in[...].reshape(128, 128)).astype(BF).reshape(8, 16, 128)
    for h in range(2):
        dc_out[h * 8:(h + 1) * 8, 32:] = planes
    dc_xy = exchange(X_DC_XY, lambda o: dc_out.at[o], dc_in, xy, along_xy, at_xy)

    g_z.wait_recv()
    gx_out[...] = jnp.sum(gz_in[...].astype(F32), axis=0).astype(BF)
    g_xy = exchange(X_G_XY, lambda o: gx_out, gx_in, xy, along_xy, at_xy)

    dc_xy.wait_recv()
    theirs = pl.ds(pl.multiple_of((1 - half) * 16, 16), 16)
    ours = pl.ds(pl.multiple_of(half * 16, 16), 16)
    c_core = swap_cores(X_C_CORE, dc_in.at[:, 32:48], c_far)
    d_core = swap_cores(X_D_CORE, dc_in.at[:, theirs], d_far)

    def deepen(group, modes_of):
        deep = dot(modes_of.reshape(128, 128), zblock[...], TN)
        for i in range(4):
            pair = [deep[:, (2 * i + h) * 128:(2 * i + h + 1) * 128].reshape(16, 8, 128) for h in range(2)]
            rows = pl.ds(pl.multiple_of(group * 64 + i * 16, 16), 16)
            zspec[:, rows, :] = jnp.concatenate(pair, axis=1).astype(BF)

    get_zblock.wait()
    for h in range(2):
        deepen(h * 2 + half, dc_in[h * 8:(h + 1) * 8, 32:])
    get_widen.wait()
    y_taps = y_taps.reshape(2, 2, 8, 128)
    y_mine = jnp.where(half == 0, y_taps[:, 0], y_taps[:, 1]).reshape(16, 1, 128)
    y_far = jnp.where(half == 0, y_taps[:, 1], y_taps[:, 0]).reshape(16, 1, 128)

    def core_part(rows, weights, first):
        for r in range(RX):
            cols = slice(r * 128, (r + 1) * 128)
            wide = dot(rows, widen[:, cols]).reshape(16, 16, 128) * weights
            part_sum = jnp.sum(wide, axis=0)[:9]
            out_core[:, cols] = part_sum if first else out_core[:, cols] + part_sum

    core_part(dc_in[:, ours].reshape(256, 128), y_mine, True)
    c_core.wait_recv()
    for h in range(2):
        deepen(h * 2 + 1 - half, c_far[h * 8:(h + 1) * 8])
    get_bwd.wait()
    for plane in range(2):
        for i in range(8):
            lines = dot(bwd[...], zspec[plane * 8 + i])
            out_features[i * 8:(i + 1) * 8, plane] = lines.reshape(8, 32, 128).astype(BF)

    d_core.wait_recv()
    core_part(d_far[...].reshape(256, 128), y_far, False)

    g_xy.wait_recv()
    gc_out[...] = jnp.sum(gx_in[...].astype(F32), axis=0)
    g_core = swap_cores(X_G_CORE, gc_out, gc_in)
    g_core.wait_recv()
    for which, sums in ((half, gc_out[...]), (1 - half, gc_in[...])):
        out_pair[which] = jnp.concatenate([sums[:24, :C], sums[:24, C:]], axis=0)
        out_modes[which] = sums[24:]
    for copy in sent:
        copy.wait_send()


def write_out(planes, core_rows, pair, modes, features, core, g_in, g_out, g_x, g_y, g_z, x_v, y_v, z_v, sem):
    copies = [pltpu.make_async_copy(planes.at[i * 32:(i + 1) * 32], features.at[i * 32:(i + 1) * 32], sem.at[i]) for i in range(2)]
    copies.append(pltpu.make_async_copy(core_rows, core, sem.at[2]))
    copies.append(pltpu.make_async_copy(pair.at[0], g_in, sem.at[3]))
    copies.append(pltpu.make_async_copy(pair.at[1], g_out, sem.at[4]))
    for copy in copies:
        copy.start()
    x_v[...] = modes[...].reshape(16, 128)[:, 0:32]
    y_v[...] = modes[...].reshape(16, 128)[:, 32:64]
    z_v[...] = modes[0, :, 64:80]
    for i, (src, dst) in enumerate(((x_v, g_x), (y_v, g_y), (z_v, g_z))):
        copies.append(pltpu.make_async_copy(src, dst, sem.at[5 + i]))
        copies[-1].start()
    for copy in copies:
        copy.wait()


def shards(features, cotangent, tucker_core, in_factor, out_factor, x_factor, y_factor, z_factor):
    tables = [jnp.asarray(m) for m in constants()]
    hbm = pl.BlockSpec(memory_space=pltpu.HBM)
    vmem = pl.BlockSpec(memory_space=pltpu.VMEM)
    buffers = [
        ((2, 64, 2, 32, 128), BF), ((2304, 2048), BF), ((48, 64), F32), ((48, 64), F32), ((16, 32), F32),
        ((16, 32), F32), ((8, 16), F32),
        ((256, 256), BF), ((256, 256), BF), ((32, 128), BF), ((128, 1024), BF), ((2, 128, 128), BF),
        ((256, 128), BF), ((128, 256), BF), ((128, 128), BF), ((512, 384), BF), ((128, 2048), BF),
        ((32, 256, 128), BF), ((2, 16, 16, 256), F32), ((16, 16, 256), F32), ((16, 16, 256), BF), ((16, 16, 256), BF),
        ((8, 16, 256), BF), ((8, 16, 256), BF),
        ((128, 2048), BF), ((64, 2048), F32), ((2304, 64), F32), ((8, 384, 64), BF), ((8, 32, 384), BF), ((8, 32, 384), BF),
        ((48, 48, 64), F32), ((8, 16, 128), BF), ((8, 16, 128), BF),
        ((2, 32, 128), F32), ((32, 128), F32), ((32, 128), BF), ((8, 32, 128), BF), ((32, 128), BF),
        ((16, 32, 128), BF), ((32, 128), F32), ((32, 128), F32),
        ((16, 48, 128), BF), ((16, 48, 128), BF), ((16, 16, 128), BF), ((16, 16, 128), BF),
        ((16, 256, 128), BF),
    ]
    factors = (in_factor, out_factor, x_factor, y_factor, z_factor)
    operands = [features, cotangent, tucker_core] + [a.T for a in factors] + tables
    results = pl.pallas_call(
        kernel,
        out_shape=(
            pltpu.VMEM((C, 2, 32, NZ), BF),
            pltpu.VMEM((9, 2048), F32),
            pltpu.VMEM((2, RIN, C), F32),
            pltpu.VMEM((2, 8, 128), F32),
        ),
        in_specs=[hbm] * (8 + len(tables)),
        out_specs=(vmem, vmem, vmem, vmem),
        scratch_shapes=[pltpu.VMEM(shape, dtype) for shape, dtype in buffers] + [
            pltpu.SemaphoreType.DMA((24,)),
            pltpu.SemaphoreType.DMA((12,)),
            pltpu.SemaphoreType.DMA((12,)),
        ],
        compiler_params=pltpu.CompilerParams(
            collective_id=0, has_side_effects=True, vmem_limit_bytes=32 * 1024 * 1024
        ),
    )(*[pltpu.with_memory_space_constraint(a, pltpu.HBM) for a in operands])
    outs = pl.pallas_call(
        write_out,
        out_shape=(
            jax.ShapeDtypeStruct((C, 2, 32, NZ), BF),
            jax.ShapeDtypeStruct((9, 2048), F32),
            jax.ShapeDtypeStruct((RIN, C), F32),
            jax.ShapeDtypeStruct((ROUT, C), F32),
            jax.ShapeDtypeStruct((RX, KX), F32),
            jax.ShapeDtypeStruct((RY, KY), F32),
            jax.ShapeDtypeStruct((RZ, KZ), F32),
        ),
        in_specs=[vmem] * 4,
        out_specs=[hbm] * 7,
        scratch_shapes=[
            pltpu.VMEM((RX, KX), F32), pltpu.VMEM((RY, KY), F32), pltpu.VMEM((RZ, KZ), F32),
            pltpu.SemaphoreType.DMA((8,)),
        ],
    )(*[pltpu.with_memory_space_constraint(a, pltpu.VMEM) for a in results])
    return outs[0], outs[1], outs[2].T, outs[3].T, outs[4].T, outs[5].T, outs[6].T


def solution(mesh):
    placed = (P(None, "px", "py", None), P(None, "px", "py", None), P(), P(), P(), P(), P(), P())
    return jax.shard_map(
        shards,
        mesh=mesh,
        in_specs=placed,
        out_specs=(P(None, "px", "py", None), P(("px", "py"), None), P(), P(), P(), P(), P()),
        check_vma=False,
    )
```

```python
import math

import jax
import jax.numpy as jnp
import numpy as np
from jax import lax
from jax.experimental import pallas as pl
from jax.experimental.pallas import tpu as pltpu
from jax.sharding import PartitionSpec as P

NX = 128
NY = 128
NZ = 128
KX = 32
KY = 32
KZ = 16
RIN = 48
ROUT = 48
RX = 16
RY = 16
RZ = 8
C = 64

BF = jnp.bfloat16
F32 = jnp.float32
MESH = pl.DeviceIdType.MESH
EXACT = lax.Precision.HIGHEST
NN = (((1,), (0,)), ((), ()))
NT = (((1,), (1,)), ((), ()))
TN = (((0,), (0,)), ((), ()))


def table(count, length):
    half = count // 2
    rows = np.arange(count)[:, None]
    cols = np.arange(length)[None, :]
    freq = np.where(rows < half, rows, rows - half + 1)
    angle = (freq * cols % length) * (2.0 * math.pi / length)
    values = np.where(rows < half, np.cos(angle), np.sin(angle)) * math.sqrt(2.0 / length)
    return values.astype(np.float32)


def two_parts(values):
    high = values.astype(jnp.bfloat16)
    low = (values - high.astype(np.float32)).astype(jnp.bfloat16)
    return high, low


def constants():
    ex, ey, ez = table(KX, NX), table(KY, NY), table(KZ, NZ)
    eye8 = np.eye(8, dtype=np.float32)
    strips = ey.reshape(KY, 4, 32).transpose(1, 0, 2)
    fwd = np.einsum("pjy,cd->pjcdy", strips, eye8).reshape(4, 256, 256)
    bwd = np.ascontiguousarray(fwd.transpose(0, 2, 1))
    z_high, z_low = two_parts(ez)
    z_rows = np.concatenate([z_high, z_low], 0)
    z_block = np.einsum("kz,ij->ikjz", z_high.astype(np.float32), eye8).reshape(128, 1024)
    planes = ex.reshape(KX, 2, 8, 4, 2)
    eye2 = np.eye(2, dtype=np.float32)
    gather = np.einsum("ayzxp,mn->pmaznyx", planes, eye2).reshape(2, 64, 128)
    gather = np.concatenate(two_parts(gather), 1)
    spread = np.einsum("ayzxp,mn->znyxpma", planes, eye2).reshape(128, 128)
    spread = np.concatenate(two_parts(spread), 0)
    swap = np.zeros((8, 2, 8, 8, 16), np.float32)
    for z in range(8):
        for n in range(2):
            for m in range(8):
                swap[z, n, m, m, 2 * z + n] = 1.0
    swap = swap.reshape(128, 128)
    swap_add = np.concatenate([swap, swap], 1)
    rows9 = np.zeros((2, 8, 2, 16, 2, 192), np.float32)
    for h in range(2):
        for m in range(8):
            for c in range(2):
                for q in range(9):
                    rows9[h, m, c, q, m // 4, (m % 4) * 36 + (h * 2 + c) * 9 + q] = 1.0
    widen = np.zeros((RX, RZ, RX, RY, RZ), np.float32)
    for r in range(RX):
        for t in range(RZ):
            widen[r, t, r, :, t] = 1.0
    mats = (
        fwd, bwd, z_rows, z_block, gather, spread, swap_add, np.ascontiguousarray(swap.T),
        rows9.reshape(512, 384), widen.reshape(128, 2048),
    )
    return [np.asarray(m).astype(jnp.bfloat16) for m in mats]


(
    X_A_CORE, X_A_XY, X_A_Z, X_D_Z, X_C_Z, X_DC_XY, X_D_CORE, X_C_CORE,
    X_G_SPLIT, X_G_Z, X_G_XY, X_G_CORE,
) = range(12)


def iota(shape, dim):
    return lax.broadcasted_iota(jnp.int32, shape, dim)


def flag(mask):
    return jnp.where(mask, 1.0, 0.0).astype(F32)


def dot(a, b, dims=NN, precision=None):
    return lax.dot_general(a, b, dims, precision=precision, preferred_element_type=F32)


def kernel(
    feat, cot, core, fin, fout, fx, fy, fz,
    k_fwd, k_bwd, k_zrows, k_zblock, k_gather, k_spread, k_swap, k_swapt, k_rows9, k_widen,
    out_features, out_core, out_pair, out_modes,
    field, core_v, fin_v, fout_v, fx_v, fy_v, fz_v,
    fwd, bwd, zrows, zblock, gather, spread, swap, swapt, rows9, widen,
    yspec, part, core_in, a_out, a_in, az_out, az_in,
    modes, x_wide, uvt, uvp, d_out, d_in, w_all, c_out, c_in,
    g_out, gs_in, gz_out, gz_in, gx_out, gx_in, gc_out, gc_in,
    dc_out, dc_in, d_far, c_far,
    zspec, local_sem, send_sem, recv_sem,
):
    px = lax.axis_index("px")
    py = lax.axis_index("py")
    x4 = lax.rem(px, 4)
    z = lax.rem(px // 4, 8)
    y_lo = px // 32
    yx = y_lo * 4 + x4
    y_hi = py // 2
    half = lax.rem(py, 2)
    y = y_hi * 2 + y_lo
    xy = y * 4 + x4
    other_core = (px, y_hi * 2 + 1 - half)

    def at_z(other):
        return (y_lo * 32 + other * 4 + x4, py)

    def at_xy(other):
        there = lax.rem(other, 8)
        return (there // 4 * 32 + z * 4 + lax.rem(there, 4), other // 8 * 2 + half)

    along_z = [lax.rem(z + d, 8) for d in (4, 3, 5, 2, 6, 1, 7)]
    along_xy = [
        lax.rem(y + dy, 4) * 4 + lax.rem(x4 + dx, 4)
        for dy, dx in (
            (2, 2), (2, 1), (2, 3), (1, 2), (3, 2), (2, 0), (0, 2), (1, 1),
            (1, 3), (3, 1), (3, 3), (1, 0), (3, 0), (0, 1), (0, 3),
        )
    ]

    loads = []

    def load(src, dst):
        copy = pltpu.make_async_copy(src, dst, local_sem.at[len(loads)])
        copy.start()
        loads.append(copy)
        return copy

    get_fwd = load(k_fwd.at[py], fwd)
    get_field = [
        [load(src.at[i * 16:(i + 1) * 16], field.at[f, i * 16:(i + 1) * 16]) for f, src in enumerate((feat, cot))]
        for i in range(4)
    ]

    barrier = pltpu.get_barrier_semaphore()
    for other in along_z:
        pl.semaphore_signal(barrier, inc=1, device_id=at_z(other), device_id_type=MESH)
    for other in along_xy:
        pl.semaphore_signal(barrier, inc=1, device_id=at_xy(other), device_id_type=MESH)
    pl.semaphore_signal(barrier, inc=1, device_id=other_core, device_id_type=MESH)

    get_zrows = load(k_zrows, zrows)
    get_small = [load(s, d) for s, d in ((fin, fin_v), (fout, fout_v), (fx, fx_v), (fy, fy_v), (fz, fz_v))]
    get_swap = load(k_swap, swap)
    get_gather = load(k_gather, gather)
    get_core = load(core, core_v)
    get_spread = load(k_spread, spread)
    get_rows9 = load(k_rows9, rows9)
    get_swapt = load(k_swapt, swapt)
    get_zblock = load(k_zblock, zblock)
    get_bwd = load(k_bwd.at[py], bwd)
    get_widen = load(k_widen, widen)

    sent = []

    def descriptor(number, src, dst, device):
        return pltpu.make_async_remote_copy(
            src_ref=src, dst_ref=dst, send_sem=send_sem.at[number], recv_sem=recv_sem.at[number],
            device_id=device, device_id_type=MESH,
        )

    def swap_cores(number, src, dst):
        copy = descriptor(number, src, dst, other_core)
        copy.start()
        sent.append(copy)
        return copy

    def exchange(number, src_of, into, mine, others, device_of):
        for other in others:
            descriptor(number, src_of(other), into.at[mine], device_of(other)).start()
        into[mine] = src_of(mine)[...]
        blocks = into.at[0:len(others)]
        whole = descriptor(number, blocks, blocks, other_core)
        sent.append(whole)
        return whole

    get_fwd.wait()
    for i in range(4):
        for f in range(2):
            get_field[i][f].wait()

            def lines(plane, carry, i=i, f=f):
                pair = []
                for h in range(2):
                    c = i * 16 + h * 8
                    block = field[f, c:c + 8, plane].reshape(256, NZ)
                    pair.append(dot(fwd[...], block).reshape(KY, 8, NZ))
                rows = pl.ds(pl.multiple_of(plane * 128 + f * 64 + i * 16, 16), 16)
                yspec[:, rows, :] = jnp.concatenate(pair, axis=1).astype(BF)
                return carry

            lax.fori_loop(0, 2, lines, 0, unroll=True)
    get_zrows.wait()

    def depth(c, h):
        def one(i, carry):
            both = dot(zrows[...], yspec[(h * 2 + c) * 8 + i], NT)
            part[c, h * 8 + i] = (both[:KZ] + both[KZ:]).astype(BF)
            return carry

        lax.fori_loop(0, 8, one, 0, unroll=4)

    for h in range(2):
        depth(1 - half, h)
    pl.semaphore_wait(barrier, 23)
    a_core = swap_cores(X_A_CORE, part.at[1 - half], core_in)
    for h in range(2):
        depth(half, h)

    a_core.wait_recv()
    a_out[...] = (part[half].astype(F32) + core_in[...].astype(F32)).astype(BF)
    a_xy = exchange(X_A_XY, lambda o: a_out.at[o], a_in, xy, along_xy, at_xy)

    for copy in get_small:
        copy.wait()
    fin_t = dot(fin_v[...], flag(lax.rem(iota((C, 128), 1), C) == iota((C, 128), 0)), NN, EXACT)
    fout_t = fout_v[...]
    b_mode = py * 8 + yx
    y_rows = dot(flag(iota((64, KY), 1) == b_mode), fy_v[...], NT, EXACT)
    z_rows = dot(flag(iota((64, KZ), 1) == 2 * z + iota((64, KZ), 0) // 32), fz_v[...], NT, EXACT)
    y_wide = flag(iota((RY, 128), 1) // RZ == iota((RY, 128), 0))
    z_wide = flag(lax.rem(iota((RZ, 128), 1), RZ) == iota((RZ, 128), 0))
    y_lane = dot(y_rows, y_wide, NN, EXACT)
    z_lane = dot(z_rows, z_wide, NN, EXACT)
    yz_lane = y_lane * z_lane
    x_rep = dot(flag(iota((64, KX), 1) == lax.rem(iota((64, KX), 0), KX)), fx_v[...], NT, EXACT)
    for r in range(RX):
        x_wide[:, r * 128:(r + 1) * 128] = jnp.broadcast_to(x_rep[:, r:r + 1], (64, 128))
        column = x_wide[:, r * 128:(r + 1) * 128] * yz_lane
        high = column.astype(BF)
        modes[:64, r * 128:(r + 1) * 128] = high
        modes[64:, r * 128:(r + 1) * 128] = (column - high.astype(F32)).astype(BF)
    x_cols = dot(fx_v[...], flag(lax.rem(iota((KX, 64), 1), KX) == iota((KX, 64), 0)), NN, EXACT)
    x_cols = jnp.concatenate([x_cols, x_cols], axis=0)
    x_cols = jnp.where(iota((32, 64), 0) // RX == iota((32, 64), 1) // KX, x_cols, 0.0)
    x_high = x_cols.astype(BF)
    x_parts = jnp.concatenate([x_cols, x_cols - x_high.astype(F32)], axis=0).astype(BF)
    z_taps = dot(flag(iota((256, KZ), 0) // RX == iota((256, KZ), 1)), fz_v[...], NT, EXACT)
    z_taps = dot(z_taps, z_wide, NN, EXACT)
    z_taps = jnp.where(lax.rem(iota((256, 128), 0), RX) == iota((256, 128), 1) // RZ, z_taps, 0.0)
    z_high = z_taps.astype(BF)
    z_parts = jnp.concatenate([z_taps, z_taps - z_high.astype(F32)], axis=1).astype(BF)
    y_taps = dot(fy_v[...], y_wide, TN, EXACT)
    for block in range(8):
        for m in range(2):
            uvp[block, m * 192 + 144:(m + 1) * 192, :] = jnp.zeros((48, 64), BF)

    get_swap.wait()
    a_xy.wait_recv()
    az_out[...] = dot(swap[...], a_in[...].reshape(256, 256)).astype(BF).reshape(8, 16, 256)
    a_z = exchange(X_A_Z, lambda o: az_out.at[o], az_in, z, along_z, at_z)

    get_core.wait()
    for g in range(8):
        both = dot(core_v[g * 288:(g + 1) * 288, :], modes[...], NT)
        w_all[g * 6:(g + 1) * 6] = (both[:, :64] + both[:, 64:]).reshape(6, 48, 64)

    get_gather.wait()
    a_z.wait_recv()
    slabs = az_in[...].reshape(128, 256)
    both = dot(gather[0], slabs[:, :128]) + dot(gather[1], slabs[:, 128:])
    spec = both[:64] + both[64:]
    spec_t = spec.T

    u_t = dot(fin_t[:, :C], spec_t[:C], NN, EXACT)
    v_t = dot(fout_t, spec_t[C:], NN, EXACT)
    for g in range(16):
        rows = u_t[g * 3:(g + 1) * 3][:, None, :] * v_t[None, :, :]
        rows = rows.reshape(144, 64)
        uvt[g * 144:(g + 1) * 144, :] = rows
        uvp[g % 8, (g // 8) * 192:(g // 8) * 192 + 144, :] = rows.astype(BF)
    for g in range(8):
        flow = dot(x_parts, uvp[g], NT)
        d_out[g] = (flow[:32] + flow[32:]).astype(BF)
    d_z = exchange(X_D_Z, lambda o: d_out.at[o], d_in, z, along_z, at_z)

    weight = w_all[...]
    h_t = jnp.sum(weight * v_t[None, :, :], axis=1)
    pulled = dot(h_t, fin_t, TN, EXACT)
    lane = iota((64, 128), 1)
    pulled = jnp.concatenate(
        [jnp.where(lane < C, pulled, 0.0), jnp.where(lane >= C, pulled, 0.0)], axis=0
    ).astype(BF)
    get_spread.wait()
    synth = dot(spread[...], pulled)
    c_out[...] = (synth[:128] + synth[128:]).astype(BF).reshape(8, 16, 128)
    c_z = exchange(X_C_Z, lambda o: c_out.at[o], c_in, z, along_z, at_z)

    g_t = jnp.sum(weight * u_t[:, None, :], axis=0)
    for f, ranks in enumerate((h_t, g_t)):
        grad = dot(ranks, spec[:, f * C:(f + 1) * C], NN, EXACT)
        g_out[f, :24] = jnp.concatenate([grad[:24], grad[24:]], axis=1)

    uv = uvt[...].T.astype(BF)
    x_sum = jnp.zeros((64, 128), F32)
    yz_sum = jnp.zeros((64, 128), F32)
    for g in range(8):
        flow = dot(uv, core_v[:, g * 256:(g + 1) * 256])
        for h in range(2):
            r = g * 2 + h
            piece = flow[:, h * 128:(h + 1) * 128]
            x_sum = x_sum + jnp.where(lane == r, jnp.sum(piece * yz_lane, axis=1, keepdims=True), 0.0)
            yz_sum = yz_sum + piece * x_wide[:, r * 128:(r + 1) * 128]
    row16 = iota((16, 128), 0)
    lane16 = iota((16, 128), 1)
    modes_grad = dot(
        flag(iota((16, 128), 0) == iota((16, 128), 1)), x_sum[:32] + x_sum[32:], NT, EXACT
    )
    modes_grad = jnp.concatenate([modes_grad, jnp.zeros((16, 96), F32)], axis=1)
    y_sum = jnp.sum(yz_sum * z_lane, axis=0, keepdims=True)
    y_pick = flag(iota((16, 128), 1) // RZ == row16)
    y_col = jnp.sum(y_pick * y_sum, axis=1, keepdims=True)
    modes_grad = modes_grad + jnp.where(lane16 == 32 + b_mode, y_col, 0.0)
    z_pick = flag(lax.rem(iota((16, 128), 1), RZ) == row16)
    z_sum = yz_sum * y_lane
    for n in range(2):
        z_col = jnp.sum(z_pick * jnp.sum(z_sum[n * 32:(n + 1) * 32], axis=0, keepdims=True), axis=1, keepdims=True)
        modes_grad = modes_grad + jnp.where(lane16 == 64 + 2 * z + n, z_col, 0.0)
    for f in range(2):
        g_out[f, 24:] = modes_grad[f * 8:(f + 1) * 8]
    g_split = swap_cores(X_G_SPLIT, g_out.at[1 - half], gs_in)
    g_split.wait_recv()
    gz_out[...] = (g_out[half] + gs_in[...]).astype(BF)
    g_z = exchange(X_G_Z, lambda o: gz_out, gz_in, z, along_z, at_z)

    d_z.wait_recv()
    taps = dot(d_in[...].reshape(256, 384), z_parts, TN)
    taps = (taps[:, :128] + taps[:, 128:]).astype(BF)
    get_rows9.wait()
    dc_out[:, :32] = dot(rows9[...], taps).astype(BF).reshape(16, 32, 128)

    get_swapt.wait()
    c_z.wait_recv()
    planes = dot(swapt[...], c_in[...].reshape(128, 128)).astype(BF).reshape(8, 16, 128)
    for h in range(2):
        dc_out[h * 8:(h + 1) * 8, 32:] = planes
    dc_xy = exchange(X_DC_XY, lambda o: dc_out.at[o], dc_in, xy, along_xy, at_xy)

    g_z.wait_recv()
    gx_out[...] = jnp.sum(gz_in[...].astype(F32), axis=0).astype(BF)
    g_xy = exchange(X_G_XY, lambda o: gx_out, gx_in, xy, along_xy, at_xy)

    dc_xy.wait_recv()
    theirs = pl.ds(pl.multiple_of((1 - half) * 16, 16), 16)
    ours = pl.ds(pl.multiple_of(half * 16, 16), 16)
    c_core = swap_cores(X_C_CORE, dc_in.at[:, 32:48], c_far)
    d_core = swap_cores(X_D_CORE, dc_in.at[:, theirs], d_far)

    def deepen(group, modes_of):
        deep = dot(modes_of.reshape(128, 128), zblock[...], TN)
        for i in range(4):
            pair = [deep[:, (2 * i + h) * 128:(2 * i + h + 1) * 128].reshape(16, 8, 128) for h in range(2)]
            rows = pl.ds(pl.multiple_of(group * 64 + i * 16, 16), 16)
            zspec[:, rows, :] = jnp.concatenate(pair, axis=1).astype(BF)

    get_zblock.wait()
    for h in range(2):
        deepen(h * 2 + half, dc_in[h * 8:(h + 1) * 8, 32:])
    get_widen.wait()
    y_taps = y_taps.reshape(2, 2, 8, 128)
    y_mine = jnp.where(half == 0, y_taps[:, 0], y_taps[:, 1]).reshape(16, 1, 128)
    y_far = jnp.where(half == 0, y_taps[:, 1], y_taps[:, 0]).reshape(16, 1, 128)

    def core_part(rows, weights, first):
        for r in range(RX):
            cols = slice(r * 128, (r + 1) * 128)
            wide = dot(rows, widen[:, cols]).reshape(16, 16, 128) * weights
            part_sum = jnp.sum(wide, axis=0)[:9]
            out_core[:, cols] = part_sum if first else out_core[:, cols] + part_sum

    core_part(dc_in[:, ours].reshape(256, 128), y_mine, True)
    c_core.wait_recv()
    for h in range(2):
        deepen(h * 2 + 1 - half, c_far[h * 8:(h + 1) * 8])
    get_bwd.wait()
    for plane in range(2):
        for i in range(8):
            lines = dot(bwd[...], zspec[plane * 8 + i])
            out_features[i * 8:(i + 1) * 8, plane] = lines.reshape(8, 32, 128).astype(BF)

    d_core.wait_recv()
    core_part(d_far[...].reshape(256, 128), y_far, False)

    g_xy.wait_recv()
    gc_out[...] = jnp.sum(gx_in[...].astype(F32), axis=0)
    g_core = swap_cores(X_G_CORE, gc_out, gc_in)
    g_core.wait_recv()
    for which, sums in ((half, gc_out[...]), (1 - half, gc_in[...])):
        out_pair[which] = jnp.concatenate([sums[:24, :C], sums[:24, C:]], axis=0)
        out_modes[which] = sums[24:]
    for copy in sent:
        copy.wait_send()


def write_out(planes, core_rows, pair, modes, features, core, g_in, g_out, g_x, g_y, g_z, x_v, y_v, z_v, sem):
    copies = [pltpu.make_async_copy(planes.at[i * 32:(i + 1) * 32], features.at[i * 32:(i + 1) * 32], sem.at[i]) for i in range(2)]
    copies.append(pltpu.make_async_copy(core_rows, core, sem.at[2]))
    copies.append(pltpu.make_async_copy(pair.at[0], g_in, sem.at[3]))
    copies.append(pltpu.make_async_copy(pair.at[1], g_out, sem.at[4]))
    for copy in copies:
        copy.start()
    x_v[...] = modes[...].reshape(16, 128)[:, 0:32]
    y_v[...] = modes[...].reshape(16, 128)[:, 32:64]
    z_v[...] = modes[0, :, 64:80]
    for i, (src, dst) in enumerate(((x_v, g_x), (y_v, g_y), (z_v, g_z))):
        copies.append(pltpu.make_async_copy(src, dst, sem.at[5 + i]))
        copies[-1].start()
    for copy in copies:
        copy.wait()


def shards(features, cotangent, tucker_core, in_factor, out_factor, x_factor, y_factor, z_factor):
    tables = [jnp.asarray(m) for m in constants()]
    hbm = pl.BlockSpec(memory_space=pltpu.HBM)
    vmem = pl.BlockSpec(memory_space=pltpu.VMEM)
    buffers = [
        ((2, 64, 2, 32, 128), BF), ((2304, 2048), BF), ((48, 64), F32), ((48, 64), F32), ((16, 32), F32),
        ((16, 32), F32), ((8, 16), F32),
        ((256, 256), BF), ((256, 256), BF), ((32, 128), BF), ((128, 1024), BF), ((2, 128, 128), BF),
        ((256, 128), BF), ((128, 256), BF), ((128, 128), BF), ((512, 384), BF), ((128, 2048), BF),
        ((32, 256, 128), BF), ((2, 16, 16, 256), BF), ((16, 16, 256), BF), ((16, 16, 256), BF), ((16, 16, 256), BF),
        ((8, 16, 256), BF), ((8, 16, 256), BF),
        ((128, 2048), BF), ((64, 2048), F32), ((2304, 64), F32), ((8, 384, 64), BF), ((8, 32, 384), BF), ((8, 32, 384), BF),
        ((48, 48, 64), F32), ((8, 16, 128), BF), ((8, 16, 128), BF),
        ((2, 32, 128), F32), ((32, 128), F32), ((32, 128), BF), ((8, 32, 128), BF), ((32, 128), BF),
        ((16, 32, 128), BF), ((32, 128), F32), ((32, 128), F32),
        ((16, 48, 128), BF), ((16, 48, 128), BF), ((16, 16, 128), BF), ((16, 16, 128), BF),
        ((16, 256, 128), BF),
    ]
    factors = (in_factor, out_factor, x_factor, y_factor, z_factor)
    operands = [features, cotangent, tucker_core] + [a.T for a in factors] + tables
    results = pl.pallas_call(
        kernel,
        out_shape=(
            pltpu.VMEM((C, 2, 32, NZ), BF),
            pltpu.VMEM((9, 2048), F32),
            pltpu.VMEM((2, RIN, C), F32),
            pltpu.VMEM((2, 8, 128), F32),
        ),
        in_specs=[hbm] * (8 + len(tables)),
        out_specs=(vmem, vmem, vmem, vmem),
        scratch_shapes=[pltpu.VMEM(shape, dtype) for shape, dtype in buffers] + [
            pltpu.SemaphoreType.DMA((24,)),
            pltpu.SemaphoreType.DMA((12,)),
            pltpu.SemaphoreType.DMA((12,)),
        ],
        compiler_params=pltpu.CompilerParams(
            collective_id=0, has_side_effects=True, vmem_limit_bytes=32 * 1024 * 1024
        ),
    )(*[pltpu.with_memory_space_constraint(a, pltpu.HBM) for a in operands])
    outs = pl.pallas_call(
        write_out,
        out_shape=(
            jax.ShapeDtypeStruct((C, 2, 32, NZ), BF),
            jax.ShapeDtypeStruct((9, 2048), F32),
            jax.ShapeDtypeStruct((RIN, C), F32),
            jax.ShapeDtypeStruct((ROUT, C), F32),
            jax.ShapeDtypeStruct((RX, KX), F32),
            jax.ShapeDtypeStruct((RY, KY), F32),
            jax.ShapeDtypeStruct((RZ, KZ), F32),
        ),
        in_specs=[vmem] * 4,
        out_specs=[hbm] * 7,
        scratch_shapes=[
            pltpu.VMEM((RX, KX), F32), pltpu.VMEM((RY, KY), F32), pltpu.VMEM((RZ, KZ), F32),
            pltpu.SemaphoreType.DMA((8,)),
        ],
    )(*[pltpu.with_memory_space_constraint(a, pltpu.VMEM) for a in results])
    return outs[0], outs[1], outs[2].T, outs[3].T, outs[4].T, outs[5].T, outs[6].T


def solution(mesh):
    placed = (P(None, "px", "py", None), P(None, "px", "py", None), P(), P(), P(), P(), P(), P())
    return jax.shard_map(
        shards,
        mesh=mesh,
        in_specs=placed,
        out_specs=(P(None, "px", "py", None), P(("px", "py"), None), P(), P(), P(), P(), P()),
        check_vma=False,
    )
```
